32 devices in a mesh: gx: 8 (over y, x, core), gy: 4 (over z).
Axes of the slice: x: 2, y: 2, z: 4, core: 2. Of those that a mesh axis runs over, the one named last changes fastest.
Arguments:
- fv_state: float32 [4, 64, 64, 1024], P(None, 'gx', 'gy'), may hold values from -6 to 6
- buffer_owner: int32 [32768, 1], P(('gx', 'gy')), may hold values from 0 to 31; in each aligned block of 1024 rows (0 to 1023, 1024 to 2047, ...) at most 64 rows name the same one
- buffer_cell: int32 [32768], P(('gx', 'gy')), may hold values from 0 to 131071
- buffer_frac: float32 [3, 32768], P(None, ('gx', 'gy')), may hold values from 0 to 1
- buffer_count: int32 [32], P(('gx', 'gy')), may hold values from 341 to 1024, as said below
- sph_offset: float32 [3, 32, 16, 128], P(None, 'gx', 'gy'), may hold values from 0 to 1
- sph_vel: float32 [3, 32, 16, 128], P(None, 'gx', 'gy'), may hold values from -6 to 6
- sph_press: float32 [32, 16, 128], P('gx', 'gy'), may hold values from 0.1 to 1
- tile_count: int32 [32, 16], P('gx', 'gy'), may hold values from 64 to 128
Outputs:
- fv_next: float32 [4, 64, 64, 1024], P(None, 'gx', 'gy')
- buffer_state: float32 [4, 32768], P(None, ('gx', 'gy'))
- sph_accel: float32 [3, 32, 16, 128], P(None, 'gx', 'gy')
The draws below stay inside these ranges and needn't reach their ends.
Inputs may be any that keep to these rules, and one draw needn't show every extreme that they name: `buffer_owner`: among the 1024 rows of one device, no owner is named by more than 64 rows, a bound that some block reaches. `buffer_count`: the live buffer slots of a device are its first ones; some device has 1024 live slots and some has 341. `tile_count`: the live particles of a tile occupy its first slots.
All inputs are finite; a program needn't handle non-finite values.
Results may differ from the reference program's by a relative error of at most 0.0003.
Values sent between devices are 32-bit elements; how exact they have to be, the bound alone decides.
A program may use at most 256 MiB of HBM per device.

```python
import math
import jax
import jax.numpy as jnp
import numpy as np
from jax import lax

CX = 8
CY = 16
CZ = 1024
BUF_DEV = 1024
PT = 128
NX = 64
NY = 64
NBUF = 32768
CAP = 64
NTX = 32
NTY = 16
N_GX = 8
N_GY = 4
DEVICES = 32


def draw_buffer_count(key, part):
    first_key, second_key = jax.random.split(jax.random.fold_in(key, 11))
    counts = jax.random.randint(first_key, (DEVICES,), BUF_DEV // 3, BUF_DEV + 1)
    order = jax.random.permutation(second_key, DEVICES)
    counts = counts.at[order[0]].set(BUF_DEV).at[order[1]].set(BUF_DEV // 3)
    return counts.astype(jnp.int32)


def with_ends(values, own_key, least, largest):
    extent = values.shape
    place = [jax.random.randint(jax.random.fold_in(own_key, axis), (), 0, extent[axis]) for axis in range(len(extent))]
    values = values.at[tuple(place)].set(least)
    longest = extent.index(max(extent))
    place[longest] = (place[longest] + 1) % extent[longest]
    return values.at[tuple(place)].set(largest)


def shard_levels(key, extent, cuts, low, high):
    def one(dim, parts):
        steps = jax.random.uniform(jax.random.fold_in(jax.random.fold_in(key, 6), dim), (parts,), jnp.float32, low / len(cuts), high / len(cuts))
        return jnp.repeat(jnp.exp(steps), extent[dim] // parts).reshape((-1,) + (1,) * (len(extent) - dim - 1))

    factor_of = one(*cuts[0])
    for cut in cuts[1:]:
        factor_of = factor_of * one(*cut)
    return factor_of


def routed_block(own_key, own, number, rows, amount, top, bound, lean):
    order = jax.random.permutation(own_key, amount)
    crowded, ordinary = shares(amount, rows * top, bound, lean, True), shares(amount, rows * top, bound, lean, False)
    places = jnp.arange(amount)

    def named(tallies, turn):
        used = int((tallies > 0).sum())
        fixed = max(1, used // 4)
        passed = fixed + (places - fixed + turn * (used - fixed)) % max(1, amount - fixed)
        return jnp.zeros((amount,), jnp.int32).at[order[jnp.where(places < fixed, places, passed)]].set(jnp.asarray(tallies, jnp.int32))

    tallies = jnp.where(number % 4 == 0, named(crowded, number // 4), named(ordinary, number - number // 4 - 1))
    mixed = jax.random.permutation(jax.random.fold_in(own, 3), amount)
    source_of, taker = mixed[0:amount // 2 * 2:2], mixed[1:amount // 2 * 2:2]
    margin = jnp.minimum(tallies[source_of] - 1, bound - tallies[taker]) // 2
    margin = jnp.where((source_of == order[0]) | (taker == order[0]) | (tallies[taker] == 0), 0, jnp.maximum(margin, 0))
    passed = jax.random.randint(jax.random.fold_in(own, 4), (amount // 2,), 0, 1 << 20) % (margin + 1)
    tallies = tallies.at[source_of].add(-passed).at[taker].add(passed)
    members = jnp.searchsorted(jnp.cumsum(tallies), jnp.arange(rows * top), side="right").astype(jnp.int32)
    table = members.reshape(top, rows).T
    table = table[jax.random.permutation(jax.random.fold_in(own, 1), rows)]
    turn = jax.random.randint(jax.random.fold_in(own, 2), (rows, 1), 0, top)
    return jnp.take_along_axis(table, (jnp.arange(top)[None, :] + turn) % top, axis=1)


def shares(count, total, most, lean, full):
    weights = [(1 << 20) // math.isqrt(grade ** lean) + 1 for grade in range(1, count + 1)]
    largest = most if full else min(most, max(-(-total // count), total * weights[0] // sum(weights)))
    least = 1 if total - largest >= count - 1 else 0
    holding, rest = [largest] + [least] * (count - 1), total - largest - least * (count - 1)
    while rest > 0:
        movable = [i for i in range(1, count) if holding[i] < largest] or [i for i in range(1, count) if holding[i] < most]
        mass, remaining = sum([weights[i] for i in movable]), rest
        for i in movable:
            extra = min(most - holding[i], max(1, remaining * weights[i] // mass), rest)
            holding[i] = holding[i] + extra
            rest = rest - extra
    return np.array(holding)


def scatter_about(stream_key, extent, spread, most, cuts=(), kind=jnp.bfloat16):
    loudness = shard_levels(stream_key, extent, cuts, -0.22, 0.18) if cuts else 1.0
    entries = jax.random.normal(stream_key, extent, jnp.float32) * spread * loudness
    return jnp.minimum(jnp.maximum(entries, -most), most).astype(kind)


def setup_inputs(seed: int = 0) -> dict:
    streams_of = jax.random.split(jax.random.key(seed), 10)
    fv_state = scatter_about(streams_of[0], (4, NX, NY, CZ), 1.0, 6.0, ((1, 8), (2, 4)), jnp.float32)
    buffer_owner_keys = jax.random.split(jax.random.fold_in(streams_of[1], 1), NBUF // BUF_DEV)
    buffer_owner_turns = jax.random.permutation(jax.random.fold_in(streams_of[1], 3), NBUF // BUF_DEV)
    buffer_owner = jax.vmap(lambda own, number: routed_block(jax.random.fold_in(streams_of[1], 2), own, number, BUF_DEV, DEVICES, 1, CAP, 2))(buffer_owner_keys, buffer_owner_turns).reshape((NBUF, 1))
    buffer_cell = with_ends(jax.random.randint(streams_of[2], (NBUF,), 0, CX * CY * CZ), jax.random.fold_in(streams_of[2], 1), 0, (CX * CY * CZ) - 1).astype(jnp.int32)
    buffer_frac = jnp.clip(1.0 * jax.random.uniform(streams_of[3], (3, NBUF), jnp.float32) ** shard_levels(streams_of[3], (3, NBUF), ((1, 32),), -0.2, 0.2), 0.0, 1.0)
    buffer_count = draw_buffer_count(jax.random.fold_in(streams_of[9], 71), 0)
    sph_offset = jnp.clip(1.0 * jax.random.uniform(streams_of[5], (3, NTX, NTY, PT), jnp.float32) ** shard_levels(streams_of[5], (3, NTX, NTY, PT), ((1, 8), (2, 4)), -0.2, 0.2), 0.0, 1.0)
    sph_vel = scatter_about(streams_of[6], (3, NTX, NTY, PT), 1.0, 6.0, ((1, 8), (2, 4)), jnp.float32)
    sph_press = jnp.clip(jnp.exp(math.log(1.0) - 2.3025851 * jax.random.uniform(streams_of[7], (NTX, NTY, PT), jnp.float32) ** shard_levels(streams_of[7], (NTX, NTY, PT), ((0, 8), (1, 4)), -0.2, 0.2)), 0.1, 1.0)
    tile_count = with_ends(jax.random.randint(streams_of[8], (NTX, NTY), 64, PT + 1), jax.random.fold_in(streams_of[8], 1), 64, PT).astype(jnp.int32)
    return dict(fv_state=fv_state, buffer_owner=buffer_owner, buffer_cell=buffer_cell, buffer_frac=buffer_frac, buffer_count=buffer_count, sph_offset=sph_offset, sph_vel=sph_vel, sph_press=sph_press, tile_count=tile_count)


STEP_RATIO = 0.3
VISCOSITY = 0.02
FORCE_SCALE = 0.1

def face_flux(left_side, right_side, normal):
    jump_term = right_side - left_side
    fluxes = [-0.5 * jump_term[channel] for channel in range(4)]
    fluxes[0] = fluxes[0] + 0.5 * (left_side[normal] + right_side[normal])
    fluxes[normal] = fluxes[normal] + 0.5 * (left_side[0] + right_side[0])
    return jnp.stack(fluxes)

def flux_step(padded):
    interior = padded[:, 1:-1, 1:-1, 1:-1]
    slab_rows = padded[:, :, 1:-1, 1:-1]
    across = face_flux(slab_rows[:, :-1], slab_rows[:, 1:], 1)
    change = across[:, 1:] - across[:, :-1]
    slab_rows = padded[:, 1:-1, :, 1:-1]
    across = face_flux(slab_rows[:, :, :-1], slab_rows[:, :, 1:], 2)
    change = change + (across[:, :, 1:] - across[:, :, :-1])
    slab_rows = padded[:, 1:-1, 1:-1, :]
    across = face_flux(slab_rows[:, :, :, :-1], slab_rows[:, :, :, 1:], 3)
    change = change + (across[:, :, :, 1:] - across[:, :, :, :-1])
    return interior - STEP_RATIO * change

def trilinear(upper, fractions, base_x, base_y, base_z):
    extent_y = upper.shape[2]
    extent_z = upper.shape[3]
    flat_field = upper.reshape(upper.shape[0], -1)
    values = jnp.zeros((upper.shape[0], base_x.shape[0]), jnp.float32)
    for corner in range(8):
        step_x = corner // 4
        step_y = corner // 2 % 2
        step_z = corner % 2
        factor_x = fractions[0] if step_x else 1.0 - fractions[0]
        factor_y = fractions[1] if step_y else 1.0 - fractions[1]
        factor_z = fractions[2] if step_z else 1.0 - fractions[2]
        position = ((base_x + step_x) * extent_y + base_y + step_y) * extent_z + base_z + step_z
        values = values + factor_x * factor_y * factor_z * jnp.take(flat_field, position, axis=1)
    return values

def pair_accel(own_tiles, other_tiles, shift_x, shift_y):
    separation_x = own_tiles[0][:, :, None] - other_tiles[0][:, None, :] - shift_x
    separation_y = own_tiles[1][:, :, None] - other_tiles[1][:, None, :] - shift_y
    separation_z = own_tiles[2][:, :, None] - other_tiles[2][:, None, :]
    distance = jnp.sqrt(separation_x * separation_x + separation_y * separation_y + separation_z * separation_z)
    closeness = jnp.maximum(1.0 - distance, 0.0)
    weight = 20.0 * closeness * closeness * closeness * other_tiles[7][:, None, :]
    push_term = (own_tiles[6][:, :, None] + other_tiles[6][:, None, :]) * weight
    weight_total = lax.optimization_barrier(jnp.sum(weight, axis=-1))
    result = []
    for channel, separation in enumerate((separation_x, separation_y, separation_z)):
        drag_term = lax.optimization_barrier(jnp.sum(weight * other_tiles[3 + channel][:, None, :], axis=-1)) - weight_total * own_tiles[3 + channel]
        result.append(lax.optimization_barrier(jnp.sum(push_term * separation, axis=-1)) + VISCOSITY * drag_term)
    return jnp.stack(result)

def reference(fv_state, buffer_owner, buffer_cell, buffer_frac, buffer_count, sph_offset, sph_vel, sph_press, tile_count):
    padded = jnp.pad(fv_state, ((0, 0), (1, 1), (1, 1), (1, 1)))

    def block_step(block_index):
        piece = lax.dynamic_slice_in_dim(padded, block_index * CX, CX + 2, 1)
        return flux_step(piece)
    blocks = lax.map(block_step, jnp.arange(N_GX, dtype=jnp.int32))
    fv_next = jnp.transpose(blocks, (1, 0, 2, 3, 4)).reshape(4, NX, NY, CZ)
    upper = jnp.pad(fv_next, ((0, 0), (0, 1), (0, 1), (0, 1)))
    owner_ids = buffer_owner[:, 0]
    cell_x = buffer_cell // (CY * CZ)
    cell_y = buffer_cell // CZ % CY
    cell_z = buffer_cell % CZ
    base_x = owner_ids // N_GY * CX + cell_x
    base_y = owner_ids % N_GY * CY + cell_y
    values = trilinear(upper, buffer_frac, base_x, base_y, cell_z)
    slot_ids = jnp.arange(NBUF, dtype=jnp.int32)
    is_live = slot_ids % BUF_DEV < buffer_count[slot_ids // BUF_DEV]
    buffer_state = jnp.where(is_live[None, :], values, 0.0)
    particle_slots = jnp.arange(PT, dtype=jnp.int32)
    tile_live = (particle_slots[None, None, :] < tile_count[:, :, None]).astype(jnp.float32)
    packed = jnp.concatenate([sph_offset, sph_vel, sph_press[None], tile_live[None]], axis=0)
    framed = jnp.pad(packed, ((0, 0), (1, 1), (1, 1), (0, 0)))

    def tile_row(row_index):
        own_tiles = lax.dynamic_index_in_dim(packed, row_index, 1, keepdims=False)
        total = jnp.zeros((3, NTY, PT), jnp.float32)
        for corner in range(9):
            step_x = corner // 3 - 1
            step_y = corner % 3 - 1
            other_row = lax.dynamic_index_in_dim(framed, row_index + 1 + step_x, 1, keepdims=False)
            other_tiles = other_row[:, 1 + step_y:1 + step_y + NTY]
            total = total + pair_accel(own_tiles, other_tiles, float(step_x), float(step_y))
        return FORCE_SCALE * total * own_tiles[7][None]
    accel_rows = lax.map(tile_row, jnp.arange(NTX, dtype=jnp.int32))
    sph_accel = jnp.transpose(accel_rows, (1, 0, 2, 3))
    return (fv_next, buffer_state, sph_accel)
```

```python
import functools

import jax
import jax.numpy as jnp
from jax import lax
from jax.experimental import pallas as pl
from jax.experimental.pallas import tpu as pltpu
from jax.sharding import PartitionSpec as P

STEP_RATIO = 0.3
VISCOSITY = 0.02
FORCE_SCALE = 0.1
LANES = 128
F32 = jnp.float32
BF16 = jnp.bfloat16


def split(value):
    high = value.astype(BF16)
    return high, (value - high.astype(F32)).astype(BF16)


def dot(left, right):
    return jnp.dot(left, right, preferred_element_type=F32)


def sweep(centre, left, right, down, up):
    length = centre.shape[-1]
    lane = lax.broadcasted_iota(jnp.int32, centre.shape[1:], 1)
    below, above = [], []
    for c in range(4):
        below.append(jnp.where(lane == 0, 0.0, pltpu.roll(centre[c], 1, 1)))
        above.append(jnp.where(lane == length - 1, 0.0, pltpu.roll(centre[c], length - 1, 1)))
    lean = [
        (right[1] - left[1]) + (up[2] - down[2]) + (above[3] - below[3]),
        right[0] - left[0],
        up[0] - down[0],
        above[0] - below[0],
    ]
    result = []
    for c in range(4):
        around = (left[c] + right[c]) + (down[c] + up[c]) + (below[c] + above[c])
        result.append(
            (1.0 - 3.0 * STEP_RATIO) * centre[c] + (0.5 * STEP_RATIO) * (around - lean[c])
        )
    return result


def sweep_block(slabs, y_low, y_up, y_up2, y_top, fv_out, high, low, keep_x, keep_y):
    cells_x, cells_y = fv_out.shape[1], fv_out.shape[2]
    length = fv_out.shape[3]
    row = lax.broadcasted_iota(jnp.int32, (cells_y, length), 0)

    def slab(x, keep):
        centre = slabs[:, x + 1]
        first = y_low[:, pl.ds(x + 1, 1), :]
        last = y_up[:, pl.ds(x + 1, 1), :]
        down = [jnp.where(row == 0, first[c], pltpu.roll(centre[c], 1, 0)) for c in range(4)]
        up = [
            jnp.where(row == cells_y - 1, last[c], pltpu.roll(centre[c], cells_y - 1, 0))
            for c in range(4)
        ]
        new = sweep(centre, slabs[:, x], slabs[:, x + 2], down, up)
        y_top[:, pl.ds(x, 1), :] = centre[:, cells_y - 1 :, :]
        for c in range(4):
            value = new[c] if keep is None else new[c] * keep
            if keep is None:
                fv_out[c, x] = value
            high[c, pl.ds(x * cells_y, cells_y), :], low[c, pl.ds(x * cells_y, cells_y), :] = split(
                value
            )

    def step(x, carry):
        slab(x, None)
        return carry

    lax.fori_loop(0, cells_x, step, 0)
    slab(cells_x, keep_x)
    rows = 16
    y_top[:, cells_x + 1 :, :] = jnp.zeros((4, rows - cells_x - 1, length), F32)
    new = sweep(
        y_up[:, 1 : 1 + rows],
        y_up[:, 0:rows],
        y_up[:, 2 : 2 + rows],
        y_top[...],
        y_up2[:, 1 : 1 + rows],
    )
    edge = lax.broadcasted_iota(jnp.int32, (rows, length), 0)
    factor = jnp.where(edge < cells_x, keep_y, jnp.where(edge == cells_x, keep_x * keep_y, 0.0))
    start = (cells_x + 1) * cells_y
    for c in range(4):
        high[c, start : start + rows, :], low[c, start : start + rows, :] = split(new[c] * factor)


def blend(index, fraction, count, base=0):
    spot = lax.broadcasted_iota(jnp.int32, (count, index.shape[1]), 0) + base
    return jnp.where(spot == index, 1.0 - fraction, jnp.where(spot == index + 1, fraction, 0.0))


def interpolate(asked, high, low, shape, put, width):
    _, cells_x, cells_y, length = shape
    rows = high.shape[1]

    def tile(t, carry):
        lanes = pl.ds(pl.multiple_of(t * width, width), width)
        cell = asked[3:4, lanes].astype(jnp.int32)
        k = cell % length
        plane = cell // length
        spot = lax.broadcasted_iota(jnp.int32, (length, width), 0)
        c = asked[2:3, lanes]
        w_high, w_low = split(blend(k, c, length))
        t_high = high[...].reshape(4 * rows, length)
        t_low = low[...].reshape(4 * rows, length)
        mixed = dot(t_high, w_high) + dot(t_low, w_high) + dot(t_high, w_low)
        weight_y = blend(plane % cells_y, asked[1:2, lanes], cells_y)
        last_y = jnp.where(plane % cells_y == cells_y - 1, asked[1:2, lanes], 0.0)
        weight_x = blend(plane // cells_y, asked[0:1, lanes], 16)
        out = []
        for channel in range(4):
            first = channel * rows
            total = jnp.zeros((cells_y, width), F32)
            for x in range(cells_x + 1):
                part = mixed[first + x * cells_y : first + (x + 1) * cells_y]
                total = total + weight_x[x : x + 1] * part
            edge = mixed[first + rows - 16 : first + rows] * weight_x
            out.append(
                jnp.sum(total * weight_y, axis=0, keepdims=True)
                + last_y * jnp.sum(edge, axis=0, keepdims=True)
            )
        put(t, jnp.concatenate(out, axis=0))
        return carry

    lax.fori_loop(0, asked.shape[1] // width, tile, 0)


def route(owner, count, devices):
    rows = owner.shape[1]
    live = lax.broadcasted_iota(jnp.int32, (1, rows), 1) < count
    place = lax.broadcasted_iota(jnp.int32, (devices, rows), 0)
    named = jnp.where((place == owner) & live, 1.0, 0.0)
    blocks = rows // LANES
    stacked = jnp.concatenate(
        [named[:, b * LANES : (b + 1) * LANES] for b in range(blocks)], axis=0
    ).astype(BF16)
    source = lax.broadcasted_iota(jnp.int32, (LANES, 2 * LANES), 0)
    target = lax.broadcasted_iota(jnp.int32, (LANES, 2 * LANES), 1)
    ladder = jnp.where((source < target) | (target >= LANES), 1.0, 0.0).astype(BF16)
    tallies = dot(stacked, ladder)
    running = jnp.zeros((devices, LANES), F32)
    ranks = []
    for b in range(blocks):
        part = tallies[b * devices : (b + 1) * devices]
        earlier = part[:, :LANES] + running
        running = running + part[:, LANES:]
        ranks.append(
            jnp.sum(earlier * named[:, b * LANES : (b + 1) * LANES], axis=0, keepdims=True)
        )
    rank = jnp.concatenate(ranks, axis=1).astype(jnp.int32)
    slot = lax.broadcasted_iota(jnp.int32, (LANES, rows), 0)
    ranked = jnp.where((slot == rank) & live, 1.0, 0.0).astype(BF16)
    return named, ranked


def pack(named, ranked, frac, cell, put):
    devices = named.shape[0]
    fields = []
    for d in range(3):
        high = frac[d : d + 1].astype(BF16).astype(F32)
        fields += [high, frac[d : d + 1] - high]
    fields += [
        (cell // 65536).astype(F32),
        (cell // 256 % 256).astype(F32),
        (cell % 256).astype(F32),
    ]
    stacked = jnp.concatenate([(named * field).astype(BF16) for field in fields], axis=0)
    sent = lax.dot_general(
        stacked, ranked, (((1,), (1,)), ((), ())), preferred_element_type=F32
    )
    part = [sent[f * devices : (f + 1) * devices] for f in range(9)]
    put(0, part[0] + part[1])
    put(1, part[2] + part[3])
    put(2, part[4] + part[5])
    put(3, part[6] * 65536.0 + part[7] * 256.0 + part[8])


def pick(named, ranked, answers):
    devices = named.shape[0]
    high, low = split(answers)
    spread = dot(high, ranked) + dot(low, ranked)
    return jnp.concatenate(
        [
            jnp.sum(spread[c * devices : (c + 1) * devices] * named, axis=0, keepdims=True)
            for c in range(4)
        ],
        axis=0,
    )


def pair_forces(tiles, put, tiles_x, tiles_y):
    slots = tiles.shape[3]
    row = lax.broadcasted_iota(jnp.int32, (8, slots), 0)

    def one(index, carry):
        m = index // tiles_y
        n = index % tiles_y
        own = tiles[m + 1, n + 1]
        sums = jnp.zeros((16, slots), F32)
        for a in range(3):
            w_high, w_low, f_high, f_low = [], [], [], []
            for b in range(3):
                other = tiles[m + a, n + b]
                shift = jnp.where(row == 0, a - 1.0, jnp.where(row == 1, b - 1.0, 0.0))
                other = other + shift
                columns = jnp.transpose(other)
                e = [own[d : d + 1] - columns[:, d : d + 1] for d in range(3)]
                s = jnp.sqrt(e[0] * e[0] + e[1] * e[1] + e[2] * e[2])
                near = jnp.maximum(1.0 - s, 0.0)
                high, low = split(near * near * near)
                w_high.append(high)
                w_low.append(low)
                masked = other * other[7:8]
                high, low = split(jnp.concatenate([masked, masked * other[6:7]], axis=0))
                f_high.append(high)
                f_low.append(low)
            w_high, w_low = jnp.concatenate(w_high, axis=0), jnp.concatenate(w_low, axis=0)
            f_high, f_low = jnp.concatenate(f_high, axis=1), jnp.concatenate(f_low, axis=1)
            both = dot(jnp.concatenate([f_high, f_low], axis=0), w_high)
            sums = sums + both[:16] + both[16:] + dot(f_high, w_low)
        result = []
        for d in range(3):
            push = (
                own[6:7] * (own[d : d + 1] * sums[7:8] - sums[d : d + 1])
                + own[d : d + 1] * sums[6:7]
                - sums[8 + d : 9 + d]
            )
            drag = sums[3 + d : 4 + d] - own[3 + d : 4 + d] * sums[7:8]
            result.append((20.0 * FORCE_SCALE) * own[7:8] * (push + VISCOSITY * drag))
        put(m, n, result)
        return carry

    lax.fori_loop(0, tiles_x * tiles_y, one, 0)


def pack_kernel(devices, owner_ref, cell_ref, frac_ref, count_ref, out_ref):
    named, ranked = route(owner_ref[...], count_ref[0], devices)

    def put(f, value):
        out_ref[:, f, :] = value

    pack(named, ranked, frac_ref[...], cell_ref[...], put)


def pick_kernel(devices, owner_ref, count_ref, answer_ref, out_ref):
    named, ranked = route(owner_ref[...], count_ref[0], devices)
    answers = jnp.concatenate([answer_ref[:, c, :] for c in range(4)], axis=0)
    out_ref[...] = pick(named, ranked, answers)


def block_kernel(slabs, y_low, y_up, y_up2, asked, fv_out, answer, high, low, y_top):
    keep_x = jnp.where(lax.axis_index("gx") < lax.axis_size("gx") - 1, 1.0, 0.0)
    keep_y = jnp.where(lax.axis_index("gy") < lax.axis_size("gy") - 1, 1.0, 0.0)
    sweep_block(slabs, y_low, y_up, y_up2, y_top, fv_out, high, low, keep_x, keep_y)
    width = 512

    def put(t, value):
        answer[:, pl.ds(pl.multiple_of(t * width, width), width)] = value

    interpolate(asked, high, low, fv_out.shape, put, width)


def sph_kernel(tiles_ref, out_ref):
    tiles_x, tiles_y = out_ref.shape[1], out_ref.shape[2]

    def put(m, n, result):
        for d in range(3):
            out_ref[d, m, pl.ds(n, 1), :] = result[d]

    pair_forces(tiles_ref, put, tiles_x, tiles_y)


def shifted(array, axis, by):
    count = lax.axis_size(axis)
    return lax.ppermute(array, axis, [(i, i + by) for i in range(count) if 0 <= i + by < count])


PARAMS = pltpu.CompilerParams(vmem_limit_bytes=48 * 1024 * 1024)
SMEM = pl.BlockSpec(memory_space=pltpu.SMEM)
VMEM = pl.BlockSpec(memory_space=pltpu.VMEM)


def per_device(
    fv_state,
    buffer_owner,
    buffer_cell,
    buffer_frac,
    buffer_count,
    sph_offset,
    sph_vel,
    sph_press,
    tile_count,
):
    devices = lax.axis_size("gx") * lax.axis_size("gy")
    _, cells_x, cells_y, length = fv_state.shape
    rows = buffer_cell.shape[0]
    capacity = 2 * rows // devices
    owner = buffer_owner.reshape(1, rows)
    cell = buffer_cell.reshape(1, rows)
    outgoing = pl.pallas_call(
        functools.partial(pack_kernel, devices),
        out_shape=jax.ShapeDtypeStruct((devices, 4, LANES), F32),
        in_specs=[VMEM, VMEM, VMEM, SMEM],
        out_specs=VMEM,
        compiler_params=PARAMS,
    )(owner, cell, buffer_frac, buffer_count)
    arrived = lax.all_to_all(
        outgoing[:, :, :capacity], ("gx", "gy"), split_axis=0, concat_axis=0, tiled=True
    )
    asked = jnp.transpose(arrived, (1, 0, 2)).reshape(4, devices * capacity)
    before = shifted(fv_state[:, -1:], "gx", 1)
    after = shifted(fv_state[:, :2], "gx", -1)
    slabs = jnp.concatenate([before, fv_state, after], axis=1)
    y_low = shifted(slabs[:, :, -1], "gy", 1)
    y_up = shifted(slabs[:, :, :2], "gy", -1)
    pad = ((0, 0), (0, 18 - cells_x - 3), (0, 0))
    fv_next, answers = pl.pallas_call(
        block_kernel,
        out_shape=(
            jax.ShapeDtypeStruct(fv_state.shape, F32),
            jax.ShapeDtypeStruct((4, devices * capacity), F32),
        ),
        in_specs=[VMEM] * 5,
        out_specs=(VMEM, VMEM),
        scratch_shapes=[
            pltpu.VMEM((4, (cells_x + 1) * cells_y + 16, length), BF16),
            pltpu.VMEM((4, (cells_x + 1) * cells_y + 16, length), BF16),
            pltpu.VMEM((4, 16, length), F32),
        ],
        compiler_params=PARAMS,
    )(slabs, y_low, jnp.pad(y_up[:, :, 0], pad), jnp.pad(y_up[:, :, 1], pad), asked)
    returned = lax.all_to_all(
        jnp.transpose(answers.reshape(4, devices, capacity), (1, 0, 2)),
        ("gx", "gy"),
        split_axis=0,
        concat_axis=0,
        tiled=True,
    )
    buffer_state = pl.pallas_call(
        functools.partial(pick_kernel, devices),
        out_shape=jax.ShapeDtypeStruct((4, rows), F32),
        in_specs=[VMEM, SMEM, VMEM],
        out_specs=VMEM,
        compiler_params=PARAMS,
    )(owner, buffer_count, jnp.pad(returned, ((0, 0), (0, 0), (0, LANES - capacity))))
    slots = sph_press.shape[2]
    live = (jnp.arange(slots, dtype=jnp.int32) < tile_count[:, :, None]).astype(F32)
    packed = jnp.concatenate([sph_offset, sph_vel, sph_press[None], live[None]], axis=0)
    packed = jnp.transpose(packed, (1, 2, 0, 3))
    packed = jnp.concatenate(
        [shifted(packed[-1:], "gx", 1), packed, shifted(packed[:1], "gx", -1)], axis=0
    )
    packed = jnp.concatenate(
        [shifted(packed[:, -1:], "gy", 1), packed, shifted(packed[:, :1], "gy", -1)], axis=1
    )
    sph_accel = pl.pallas_call(
        sph_kernel,
        out_shape=jax.ShapeDtypeStruct(sph_offset.shape, F32),
        in_specs=[VMEM],
        out_specs=VMEM,
        compiler_params=PARAMS,
    )(packed)
    return fv_next, buffer_state, sph_accel


def solution(mesh):
    return jax.shard_map(
        per_device,
        mesh=mesh,
        in_specs=(
            P(None, "gx", "gy", None),
            P(("gx", "gy"), None),
            P(("gx", "gy")),
            P(None, ("gx", "gy")),
            P(("gx", "gy")),
            P(None, "gx", "gy", None),
            P(None, "gx", "gy", None),
            P("gx", "gy", None),
            P("gx", "gy"),
        ),
        out_specs=(P(None, "gx", "gy", None), P(None, ("gx", "gy")), P(None, "gx", "gy", None)),
        check_vma=False,
    )
```

```python
import functools

import jax
import jax.numpy as jnp
from jax import lax
from jax.experimental import pallas as pl
from jax.experimental.pallas import tpu as pltpu
from jax.sharding import PartitionSpec as P

STEP_RATIO = 0.3
VISCOSITY = 0.02
FORCE_SCALE = 0.1
LANES = 128
F32 = jnp.float32
BF16 = jnp.bfloat16


def split(value):
    high = value.astype(BF16)
    return high, (value - high.astype(F32)).astype(BF16)


def dot(left, right):
    return jnp.dot(left, right, preferred_element_type=F32)


def sweep(centre, left, right, down, up):
    length = centre.shape[-1]
    lane = lax.broadcasted_iota(jnp.int32, centre.shape[1:], 1)
    below, above = [], []
    for c in range(4):
        below.append(jnp.where(lane == 0, 0.0, pltpu.roll(centre[c], 1, 1)))
        above.append(jnp.where(lane == length - 1, 0.0, pltpu.roll(centre[c], length - 1, 1)))
    lean = [
        (right[1] - left[1]) + (up[2] - down[2]) + (above[3] - below[3]),
        right[0] - left[0],
        up[0] - down[0],
        above[0] - below[0],
    ]
    result = []
    for c in range(4):
        around = (left[c] + right[c]) + (down[c] + up[c]) + (below[c] + above[c])
        result.append(
            (1.0 - 3.0 * STEP_RATIO) * centre[c] + (0.5 * STEP_RATIO) * (around - lean[c])
        )
    return result


def sweep_block(slabs, y_low, y_up, y_up2, y_top, fv_out, high, low, keep_x, keep_y):
    cells_x, cells_y = fv_out.shape[1], fv_out.shape[2]
    length = fv_out.shape[3]
    row = lax.broadcasted_iota(jnp.int32, (cells_y, length), 0)

    def slab(x, keep):
        centre = slabs[:, x + 1]
        first = y_low[:, pl.ds(x + 1, 1), :]
        last = y_up[:, pl.ds(x + 1, 1), :]
        down = [jnp.where(row == 0, first[c], pltpu.roll(centre[c], 1, 0)) for c in range(4)]
        up = [
            jnp.where(row == cells_y - 1, last[c], pltpu.roll(centre[c], cells_y - 1, 0))
            for c in range(4)
        ]
        new = sweep(centre, slabs[:, x], slabs[:, x + 2], down, up)
        y_top[:, pl.ds(x, 1), :] = centre[:, cells_y - 1 :, :]
        for c in range(4):
            value = new[c] if keep is None else new[c] * keep
            if keep is None:
                fv_out[c, x] = value
            high[c, pl.ds(x * cells_y, cells_y), :], low[c, pl.ds(x * cells_y, cells_y), :] = split(
                value
            )

    def step(x, carry):
        slab(x, None)
        return carry

    lax.fori_loop(0, cells_x, step, 0)
    slab(cells_x, keep_x)
    rows = 16
    y_top[:, cells_x + 1 :, :] = jnp.zeros((4, rows - cells_x - 1, length), F32)
    new = sweep(
        y_up[:, 1 : 1 + rows],
        y_up[:, 0:rows],
        y_up[:, 2 : 2 + rows],
        y_top[...],
        y_up2[:, 1 : 1 + rows],
    )
    edge = lax.broadcasted_iota(jnp.int32, (rows, length), 0)
    factor = jnp.where(edge < cells_x, keep_y, jnp.where(edge == cells_x, keep_x * keep_y, 0.0))
    start = (cells_x + 1) * cells_y
    for c in range(4):
        high[c, start : start + rows, :], low[c, start : start + rows, :] = split(new[c] * factor)


def blend(index, fraction, count, base=0):
    spot = lax.broadcasted_iota(jnp.int32, (count, index.shape[1]), 0) + base
    return jnp.where(spot == index, 1.0 - fraction, jnp.where(spot == index + 1, fraction, 0.0))


def interpolate(asked, high, low, shape, put, width):
    _, cells_x, cells_y, length = shape
    rows = high.shape[1]

    def tile(t, carry):
        lanes = pl.ds(pl.multiple_of(t * width, width), width)
        cell = asked[3:4, lanes].astype(jnp.int32)
        k = cell % length
        plane = cell // length
        spot = lax.broadcasted_iota(jnp.int32, (length, width), 0)
        c = asked[2:3, lanes]
        w_high, w_low = split(blend(k, c, length))
        t_high = high[...].reshape(4 * rows, length)
        t_low = low[...].reshape(4 * rows, length)
        mixed = dot(t_high, w_high) + dot(t_low, w_high) + dot(t_high, w_low)
        weight_y = blend(plane % cells_y, asked[1:2, lanes], cells_y)
        last_y = jnp.where(plane % cells_y == cells_y - 1, asked[1:2, lanes], 0.0)
        weight_x = blend(plane // cells_y, asked[0:1, lanes], 16)
        out = []
        for channel in range(4):
            first = channel * rows
            total = jnp.zeros((cells_y, width), F32)
            for x in range(cells_x + 1):
                part = mixed[first + x * cells_y : first + (x + 1) * cells_y]
                total = total + weight_x[x : x + 1] * part
            edge = mixed[first + rows - 16 : first + rows] * weight_x
            out.append(
                jnp.sum(total * weight_y, axis=0, keepdims=True)
                + last_y * jnp.sum(edge, axis=0, keepdims=True)
            )
        put(t, jnp.concatenate(out, axis=0))
        return carry

    lax.fori_loop(0, asked.shape[1] // width, tile, 0)


def route(owner, count, devices):
    rows = owner.shape[1]
    live = lax.broadcasted_iota(jnp.int32, (1, rows), 1) < count
    place = lax.broadcasted_iota(jnp.int32, (devices, rows), 0)
    named = jnp.where((place == owner) & live, 1.0, 0.0)
    blocks = rows // LANES
    stacked = jnp.concatenate(
        [named[:, b * LANES : (b + 1) * LANES] for b in range(blocks)], axis=0
    ).astype(BF16)
    source = lax.broadcasted_iota(jnp.int32, (LANES, 2 * LANES), 0)
    target = lax.broadcasted_iota(jnp.int32, (LANES, 2 * LANES), 1)
    ladder = jnp.where((source < target) | (target >= LANES), 1.0, 0.0).astype(BF16)
    tallies = dot(stacked, ladder)
    running = jnp.zeros((devices, LANES), F32)
    ranks = []
    for b in range(blocks):
        part = tallies[b * devices : (b + 1) * devices]
        earlier = part[:, :LANES] + running
        running = running + part[:, LANES:]
        ranks.append(
            jnp.sum(earlier * named[:, b * LANES : (b + 1) * LANES], axis=0, keepdims=True)
        )
    rank = jnp.concatenate(ranks, axis=1).astype(jnp.int32)
    slot = lax.broadcasted_iota(jnp.int32, (LANES, rows), 0)
    ranked = jnp.where((slot == rank) & live, 1.0, 0.0).astype(BF16)
    return named, ranked


def pack(named, ranked, frac, cell, put):
    devices = named.shape[0]
    fields = []
    for d in range(3):
        high = frac[d : d + 1].astype(BF16).astype(F32)
        fields += [high, frac[d : d + 1] - high]
    fields += [
        (cell // 65536).astype(F32),
        (cell // 256 % 256).astype(F32),
        (cell % 256).astype(F32),
    ]
    stacked = jnp.concatenate([(named * field).astype(BF16) for field in fields], axis=0)
    sent = lax.dot_general(
        stacked, ranked, (((1,), (1,)), ((), ())), preferred_element_type=F32
    )
    part = [sent[f * devices : (f + 1) * devices] for f in range(9)]
    put(0, part[0] + part[1])
    put(1, part[2] + part[3])
    put(2, part[4] + part[5])
    put(3, part[6] * 65536.0 + part[7] * 256.0 + part[8])


def pick(named, ranked, answers):
    devices = named.shape[0]
    high, low = split(answers)
    spread = dot(high, ranked) + dot(low, ranked)
    return jnp.concatenate(
        [
            jnp.sum(spread[c * devices : (c + 1) * devices] * named, axis=0, keepdims=True)
            for c in range(4)
        ],
        axis=0,
    )


def pair_forces(tiles, put, count, place):
    slots = tiles.shape[3]
    row = lax.broadcasted_iota(jnp.int32, (8, slots), 0)

    def one(index, carry):
        m, n = place(index)
        own = tiles[m + 1, n + 1]
        sums = jnp.zeros((16, slots), F32)
        for a in range(3):
            w_high, w_low, f_high, f_low = [], [], [], []
            for b in range(3):
                other = tiles[m + a, n + b]
                shift = jnp.where(row == 0, a - 1.0, jnp.where(row == 1, b - 1.0, 0.0))
                other = other + shift
                columns = jnp.transpose(other)
                e = [own[d : d + 1] - columns[:, d : d + 1] for d in range(3)]
                s = jnp.sqrt(e[0] * e[0] + e[1] * e[1] + e[2] * e[2])
                near = jnp.maximum(1.0 - s, 0.0)
                high, low = split(near * near * near)
                w_high.append(high)
                w_low.append(low)
                masked = other * other[7:8]
                high, low = split(jnp.concatenate([masked, masked * other[6:7]], axis=0))
                f_high.append(high)
                f_low.append(low)
            w_high, w_low = jnp.concatenate(w_high, axis=0), jnp.concatenate(w_low, axis=0)
            f_high, f_low = jnp.concatenate(f_high, axis=1), jnp.concatenate(f_low, axis=1)
            both = dot(jnp.concatenate([f_high, f_low], axis=0), w_high)
            sums = sums + both[:16] + both[16:] + dot(f_high, w_low)
        result = []
        for d in range(3):
            push = (
                own[6:7] * (own[d : d + 1] * sums[7:8] - sums[d : d + 1])
                + own[d : d + 1] * sums[6:7]
                - sums[8 + d : 9 + d]
            )
            drag = sums[3 + d : 4 + d] - own[3 + d : 4 + d] * sums[7:8]
            result.append((20.0 * FORCE_SCALE) * own[7:8] * (push + VISCOSITY * drag))
        put(m, n, result)
        return carry

    lax.fori_loop(0, count, one, 0)


def whole_kernel(
    grid,
    capacity,
    owner_ref,
    cell_ref,
    frac_ref,
    count_ref,
    fv,
    packed,
    fv_out,
    state_out,
    accel_out,
    slabs,
    fresh,
    stage,
    landed,
    corner_out,
    corner_in,
    y_low,
    y_up,
    y_up2,
    y_top,
    high,
    low,
    tiles,
    ask_out,
    ask_in,
    asked,
    reply_out,
    reply_in,
    near_send,
    near_recv,
    ask_send,
    ask_recv,
    reply_send,
    reply_recv,
    local_sem,
):
    grid_x, grid_y = grid
    devices = grid_x * grid_y
    gx, gy = lax.axis_index("gx"), lax.axis_index("gy")
    me = gx * grid_y + gy
    _, cells_x, cells_y, length = fresh.shape
    tiles_x, tiles_y = packed.shape[0], packed.shape[1]
    load = pltpu.make_async_copy(fv, slabs.at[:, 1 : 1 + cells_x], local_sem.at[0])
    load.start()

    for ref in (landed, corner_in, y_low, y_up, y_up2):
        ref[...] = jnp.zeros(ref.shape, ref.dtype)
    for x in (0, cells_x + 1, cells_x + 2):
        slabs[:, x] = jnp.zeros((4, cells_y, length), F32)
    for n in range(tiles_y + 2):
        tiles[0, n] = jnp.zeros(tiles.shape[2:], F32)
        tiles[tiles_x + 1, n] = jnp.zeros(tiles.shape[2:], F32)
    for m in range(tiles_x):
        tiles[m + 1, 0] = jnp.zeros(tiles.shape[2:], F32)
        tiles[m + 1, tiles_y + 1] = jnp.zeros(tiles.shape[2:], F32)
        for n in range(tiles_y):
            tiles[m + 1, n + 1] = packed[m, n]

    def everyone(action):
        def step(p, carry):
            action(lax.rem(me + p, devices))
            return carry

        lax.fori_loop(1, devices, step, 0)

    def at(device):
        return {"gx": device // grid_y, "gy": lax.rem(device, grid_y)}

    barrier = pltpu.get_barrier_semaphore()
    everyone(
        lambda other: pl.semaphore_signal(
            barrier, inc=1, device_id=at(other), device_id_type=pl.DeviceIdType.MESH
        )
    )

    named, ranked = route(owner_ref[...], count_ref[0], devices)

    def put_ask(f, value):
        ask_out[:, f, :] = value

    pack(named, ranked, frac_ref[...], cell_ref[...], put_ask)
    load.wait()
    for x in range(cells_x):
        stage[0, :, x : x + 1, :] = slabs[:, x + 1, cells_y - 1 :, :]
        stage[1, :, x : x + 1, :] = slabs[:, x + 1, 0:1, :]
        stage[2, :, x : x + 1, :] = slabs[:, x + 1, 1:2, :]
    corner_out[...] = jnp.zeros(corner_out.shape, F32)
    corner_out[0, :, 0:1, :] = slabs[:, 1, 0:1, :]
    corner_out[0, :, 1:2, :] = slabs[:, 2, 0:1, :]
    corner_out[0, :, 2:3, :] = slabs[:, 1, 1:2, :]
    corner_out[1, :, 0:1, :] = slabs[:, cells_x, 0:1, :]
    corner_out[2, :, 0:1, :] = slabs[:, 1, cells_y - 1 :, :]
    ask_in[me] = ask_out[me]

    pl.semaphore_wait(barrier, devices - 1)

    def toward(order, source, target, dx, dy):
        copy = pltpu.make_async_remote_copy(
            src_ref=source,
            dst_ref=target,
            send_sem=near_send.at[order],
            recv_sem=near_recv.at[order],
            device_id={"gx": gx + dx, "gy": gy + dy},
            device_id_type=pl.DeviceIdType.MESH,
        )

        def inside(sign):
            ok = None
            for place, count, by in ((gx, grid_x, sign * dx), (gy, grid_y, sign * dy)):
                if by:
                    one = place + by < count if by > 0 else place + by >= 0
                    ok = one if ok is None else jnp.logical_and(ok, one)
            return ok

        return copy, inside(1), inside(-1)

    tx, ty = tiles_x, tiles_y
    field = [
        (fv.at[:, cells_x - 1 : cells_x], slabs.at[:, 0:1], 1, 0),
        (fv.at[:, 0:2], slabs.at[:, cells_x + 1 : cells_x + 3], -1, 0),
        (stage.at[0], landed.at[0], 0, 1),
        (stage.at[1:3], landed.at[1:3], 0, -1),
        (corner_out.at[0], corner_in.at[0], -1, -1),
        (corner_out.at[1], corner_in.at[1], 1, -1),
        (corner_out.at[2], corner_in.at[2], -1, 1),
    ]
    particles = [
        (packed.at[tx - 1], tiles.at[0, 1 : 1 + ty], 1, 0),
        (packed.at[0], tiles.at[tx + 1, 1 : 1 + ty], -1, 0),
        (packed.at[:, ty - 1], tiles.at[1 : 1 + tx, 0], 0, 1),
        (packed.at[:, 0], tiles.at[1 : 1 + tx, ty + 1], 0, -1),
        (packed.at[tx - 1, ty - 1], tiles.at[0, 0], 1, 1),
        (packed.at[tx - 1, 0], tiles.at[0, ty + 1], 1, -1),
        (packed.at[0, ty - 1], tiles.at[tx + 1, 0], -1, 1),
        (packed.at[0, 0], tiles.at[tx + 1, ty + 1], -1, -1),
    ]
    copies = [toward(i, *one) for i, one in enumerate(field + particles)]

    def exchange(out, into, send, recv, other, source):
        return pltpu.make_async_remote_copy(
            src_ref=out.at[other],
            dst_ref=into.at[source],
            send_sem=send.at[other],
            recv_sem=recv.at[source],
            device_id=at(other),
            device_id_type=pl.DeviceIdType.MESH,
        )

    for copy, to, _ in copies[: len(field)]:
        pl.when(to)(copy.start)
    everyone(lambda other: exchange(ask_out, ask_in, ask_send, ask_recv, other, me).start())
    for copy, to, _ in copies[len(field) :]:
        pl.when(to)(copy.start)

    def put_accel(m, n, result):
        for d in range(3):
            accel_out[d, m, pl.ds(n, 1), :] = result[d]

    inner = tiles_y - 2
    pair_forces(
        tiles, put_accel, (tiles_x - 2) * inner, lambda i: (1 + i // inner, 1 + lax.rem(i, inner))
    )

    for copy, _, source in copies[: len(field)]:
        pl.when(source)(copy.wait_recv)
    y_low[:, 1 : 1 + cells_x] = landed[0]
    y_up[:, 1 : 1 + cells_x] = landed[1]
    y_up2[:, 1 : 1 + cells_x] = landed[2]
    y_up[:, cells_x + 1 : cells_x + 3] = corner_in[0, :, 0:2]
    y_up2[:, cells_x + 1 : cells_x + 2] = corner_in[0, :, 2:3]
    y_up[:, 0:1] = corner_in[1, :, 0:1]
    y_low[:, cells_x + 1 : cells_x + 2] = corner_in[2, :, 0:1]
    keep_x = jnp.where(gx < grid_x - 1, 1.0, 0.0)
    keep_y = jnp.where(gy < grid_y - 1, 1.0, 0.0)
    sweep_block(slabs, y_low, y_up, y_up2, y_top, fresh, high, low, keep_x, keep_y)
    store = pltpu.make_async_copy(fresh, fv_out, local_sem.at[1])
    store.start()

    everyone(lambda other: exchange(ask_out, ask_in, ask_send, ask_recv, me, other).wait_recv())
    share = LANES // capacity
    for q in range(devices // share):
        total = ask_in[q * share]
        for r in range(1, share):
            total = total + pltpu.roll(ask_in[q * share + r], r * capacity, 1)
        asked[:, q * LANES : (q + 1) * LANES] = total
    width = 512

    def put_reply(t, value):
        for q in range(width // LANES):
            part = value[:, q * LANES : (q + 1) * LANES]
            for r in range(share):
                turned = pltpu.roll(part, LANES - r * capacity, 1) if r else part
                reply_out[t * (width // capacity) + q * share + r] = turned

    interpolate(asked, high, low, fresh.shape, put_reply, width)
    everyone(
        lambda other: exchange(reply_out, reply_in, reply_send, reply_recv, other, me).start()
    )
    reply_in[me] = reply_out[me]

    for copy, _, source in copies[len(field) :]:
        pl.when(source)(copy.wait_recv)
    pair_forces(
        tiles, put_accel, 2 * ty, lambda i: ((i // ty) * (tiles_x - 1), lax.rem(i, ty))
    )
    pair_forces(
        tiles,
        put_accel,
        2 * (tiles_x - 2),
        lambda i: (1 + i // 2, lax.rem(i, 2) * (tiles_y - 1)),
    )

    everyone(
        lambda other: exchange(
            reply_out, reply_in, reply_send, reply_recv, me, other
        ).wait_recv()
    )
    named, ranked = route(owner_ref[...], count_ref[0], devices)
    answers = jnp.concatenate([reply_in[:, c, :] for c in range(4)], axis=0)
    state_out[...] = pick(named, ranked, answers)

    for copy, to, _ in copies:
        pl.when(to)(copy.wait_send)
    everyone(lambda other: exchange(ask_out, ask_in, ask_send, ask_recv, other, me).wait_send())
    everyone(
        lambda other: exchange(reply_out, reply_in, reply_send, reply_recv, other, me).wait_send()
    )
    store.wait()


def per_device(
    fv_state,
    buffer_owner,
    buffer_cell,
    buffer_frac,
    buffer_count,
    sph_offset,
    sph_vel,
    sph_press,
    tile_count,
):
    grid = (lax.axis_size("gx"), lax.axis_size("gy"))
    devices = grid[0] * grid[1]
    _, cells_x, cells_y, length = fv_state.shape
    rows = buffer_cell.shape[0]
    capacity = 2 * rows // devices
    tiles_x, tiles_y, slots = sph_press.shape
    live = (jnp.arange(slots, dtype=jnp.int32) < tile_count[:, :, None]).astype(F32)
    packed = jnp.concatenate([sph_offset, sph_vel, sph_press[None], live[None]], axis=0)
    packed = jnp.transpose(packed, (1, 2, 0, 3))
    table = (cells_x + 1) * cells_y + 16
    mail = pltpu.VMEM((devices, 4, LANES), F32)
    dma = pltpu.SemaphoreType.DMA
    vmem = pl.BlockSpec(memory_space=pltpu.VMEM)
    anywhere = pl.BlockSpec(memory_space=pl.ANY)
    return pl.pallas_call(
        functools.partial(whole_kernel, grid, capacity),
        out_shape=(
            jax.ShapeDtypeStruct(fv_state.shape, F32),
            jax.ShapeDtypeStruct((4, rows), F32),
            jax.ShapeDtypeStruct(sph_offset.shape, F32),
        ),
        in_specs=[vmem, vmem, vmem, pl.BlockSpec(memory_space=pltpu.SMEM), anywhere, vmem],
        out_specs=(anywhere, vmem, vmem),
        scratch_shapes=[
            pltpu.VMEM((4, cells_x + 3, cells_y, length), F32),
            pltpu.VMEM((4, cells_x, cells_y, length), F32),
            pltpu.VMEM((3, 4, cells_x, length), F32),
            pltpu.VMEM((3, 4, cells_x, length), F32),
            pltpu.VMEM((3, 4, 8, length), F32),
            pltpu.VMEM((3, 4, 8, length), F32),
            pltpu.VMEM((4, 24, length), F32),
            pltpu.VMEM((4, 24, length), F32),
            pltpu.VMEM((4, 24, length), F32),
            pltpu.VMEM((4, 16, length), F32),
            pltpu.VMEM((4, table, length), BF16),
            pltpu.VMEM((4, table, length), BF16),
            pltpu.VMEM((tiles_x + 2, tiles_y + 2, 8, slots), F32),
            mail,
            mail,
            pltpu.VMEM((4, devices * capacity), F32),
            mail,
            mail,
            dma((15,)),
            dma((15,)),
            dma((devices,)),
            dma((devices,)),
            dma((devices,)),
            dma((devices,)),
            dma((2,)),
        ],
        compiler_params=pltpu.CompilerParams(
            collective_id=0, has_side_effects=True, vmem_limit_bytes=48 * 1024 * 1024
        ),
    )(
        buffer_owner.reshape(1, rows),
        buffer_cell.reshape(1, rows),
        buffer_frac,
        buffer_count,
        fv_state,
        packed,
    )


def solution(mesh):
    return jax.shard_map(
        per_device,
        mesh=mesh,
        in_specs=(
            P(None, "gx", "gy", None),
            P(("gx", "gy"), None),
            P(("gx", "gy")),
            P(None, ("gx", "gy")),
            P(("gx", "gy")),
            P(None, "gx", "gy", None),
            P(None, "gx", "gy", None),
            P("gx", "gy", None),
            P("gx", "gy"),
        ),
        out_specs=(P(None, "gx", "gy", None), P(None, ("gx", "gy")), P(None, "gx", "gy", None)),
        check_vma=False,
    )
```

```python
import functools

import jax
import jax.numpy as jnp
from jax import lax
from jax.experimental import pallas as pl
from jax.experimental.pallas import tpu as pltpu
from jax.sharding import PartitionSpec as P

STEP_RATIO = 0.3
VISCOSITY = 0.02
FORCE_SCALE = 0.1
LANES = 128
F32 = jnp.float32
BF16 = jnp.bfloat16


def split(value):
    high = value.astype(BF16)
    return high, (value - high.astype(F32)).astype(BF16)


def dot(left, right):
    return jnp.dot(left, right, preferred_element_type=F32)


def sweep(centre, left, right, down, up):
    length = centre.shape[-1]
    lane = lax.broadcasted_iota(jnp.int32, centre.shape[1:], 1)
    below, above = [], []
    for c in range(4):
        below.append(jnp.where(lane == 0, 0.0, pltpu.roll(centre[c], 1, 1)))
        above.append(jnp.where(lane == length - 1, 0.0, pltpu.roll(centre[c], length - 1, 1)))
    lean = [
        (right[1] - left[1]) + (up[2] - down[2]) + (above[3] - below[3]),
        right[0] - left[0],
        up[0] - down[0],
        above[0] - below[0],
    ]
    result = []
    for c in range(4):
        around = (left[c] + right[c]) + (down[c] + up[c]) + (below[c] + above[c])
        result.append(
            (1.0 - 3.0 * STEP_RATIO) * centre[c] + (0.5 * STEP_RATIO) * (around - lean[c])
        )
    return result


def sweep_block(slabs, y_low, y_up, y_up2, y_top, fv_out, high, low, keep_x, keep_y):
    cells_x, cells_y = fv_out.shape[1], fv_out.shape[2]
    length = fv_out.shape[3]
    row = lax.broadcasted_iota(jnp.int32, (cells_y, length), 0)

    def slab(x, keep):
        centre = slabs[:, x + 1]
        first = y_low[:, pl.ds(x + 1, 1), :]
        last = y_up[:, pl.ds(x + 1, 1), :]
        down = [jnp.where(row == 0, first[c], pltpu.roll(centre[c], 1, 0)) for c in range(4)]
        up = [
            jnp.where(row == cells_y - 1, last[c], pltpu.roll(centre[c], cells_y - 1, 0))
            for c in range(4)
        ]
        new = sweep(centre, slabs[:, x], slabs[:, x + 2], down, up)
        y_top[:, pl.ds(x, 1), :] = centre[:, cells_y - 1 :, :]
        for c in range(4):
            value = new[c] if keep is None else new[c] * keep
            if keep is None:
                fv_out[c, x] = value
            high[c, pl.ds(x * cells_y, cells_y), :], low[c, pl.ds(x * cells_y, cells_y), :] = split(
                value
            )

    def step(x, carry):
        slab(x, None)
        return carry

    lax.fori_loop(0, cells_x, step, 0)
    slab(cells_x, keep_x)
    rows = 16
    y_top[:, cells_x + 1 :, :] = jnp.zeros((4, rows - cells_x - 1, length), F32)
    new = sweep(
        y_up[:, 1 : 1 + rows],
        y_up[:, 0:rows],
        y_up[:, 2 : 2 + rows],
        y_top[...],
        y_up2[:, 1 : 1 + rows],
    )
    edge = lax.broadcasted_iota(jnp.int32, (rows, length), 0)
    factor = jnp.where(edge < cells_x, keep_y, jnp.where(edge == cells_x, keep_x * keep_y, 0.0))
    start = (cells_x + 1) * cells_y
    for c in range(4):
        high[c, start : start + rows, :], low[c, start : start + rows, :] = split(new[c] * factor)


def blend(index, fraction, count, base=0):
    spot = lax.broadcasted_iota(jnp.int32, (count, index.shape[1]), 0) + base
    return jnp.where(spot == index, 1.0 - fraction, jnp.where(spot == index + 1, fraction, 0.0))


def interpolate(asked, high, low, shape, put, width):
    _, cells_x, cells_y, length = shape
    rows = high.shape[1]

    def tile(t, carry):
        lanes = pl.ds(pl.multiple_of(t * width, width), width)
        cell = asked[3:4, lanes].astype(jnp.int32)
        k = cell % length
        plane = cell // length
        spot = lax.broadcasted_iota(jnp.int32, (length, width), 0)
        c = asked[2:3, lanes]
        w_high, w_low = split(blend(k, c, length))
        t_high = high[...].reshape(4 * rows, length)
        t_low = low[...].reshape(4 * rows, length)
        mixed = dot(t_high, w_high) + dot(t_low, w_high) + dot(t_high, w_low)
        weight_y = blend(plane % cells_y, asked[1:2, lanes], cells_y)
        last_y = jnp.where(plane % cells_y == cells_y - 1, asked[1:2, lanes], 0.0)
        weight_x = blend(plane // cells_y, asked[0:1, lanes], 16)
        out = []
        for channel in range(4):
            first = channel * rows
            total = jnp.zeros((cells_y, width), F32)
            for x in range(cells_x + 1):
                part = mixed[first + x * cells_y : first + (x + 1) * cells_y]
                total = total + weight_x[x : x + 1] * part
            edge = mixed[first + rows - 16 : first + rows] * weight_x
            out.append(
                jnp.sum(total * weight_y, axis=0, keepdims=True)
                + last_y * jnp.sum(edge, axis=0, keepdims=True)
            )
        put(t, jnp.concatenate(out, axis=0))
        return carry

    lax.fori_loop(0, asked.shape[1] // width, tile, 0)


def route(owner, count, devices):
    rows = owner.shape[1]
    live = lax.broadcasted_iota(jnp.int32, (1, rows), 1) < count
    place = lax.broadcasted_iota(jnp.int32, (devices, rows), 0)
    named = jnp.where((place == owner) & live, 1.0, 0.0)
    blocks = rows // LANES
    stacked = jnp.concatenate(
        [named[:, b * LANES : (b + 1) * LANES] for b in range(blocks)], axis=0
    ).astype(BF16)
    source = lax.broadcasted_iota(jnp.int32, (LANES, 2 * LANES), 0)
    target = lax.broadcasted_iota(jnp.int32, (LANES, 2 * LANES), 1)
    ladder = jnp.where((source < target) | (target >= LANES), 1.0, 0.0).astype(BF16)
    tallies = dot(stacked, ladder)
    running = jnp.zeros((devices, LANES), F32)
    ranks = []
    for b in range(blocks):
        part = tallies[b * devices : (b + 1) * devices]
        earlier = part[:, :LANES] + running
        running = running + part[:, LANES:]
        ranks.append(
            jnp.sum(earlier * named[:, b * LANES : (b + 1) * LANES], axis=0, keepdims=True)
        )
    rank = jnp.concatenate(ranks, axis=1).astype(jnp.int32)
    slot = lax.broadcasted_iota(jnp.int32, (LANES, rows), 0)
    ranked = jnp.where((slot == rank) & live, 1.0, 0.0).astype(BF16)
    return named, ranked


def pack(named, ranked, frac, cell, put):
    devices = named.shape[0]
    fields = []
    for d in range(3):
        high = frac[d : d + 1].astype(BF16).astype(F32)
        fields += [high, frac[d : d + 1] - high]
    fields += [
        (cell // 65536).astype(F32),
        (cell // 256 % 256).astype(F32),
        (cell % 256).astype(F32),
    ]
    stacked = jnp.concatenate([(named * field).astype(BF16) for field in fields], axis=0)
    sent = lax.dot_general(
        stacked, ranked, (((1,), (1,)), ((), ())), preferred_element_type=F32
    )
    part = [sent[f * devices : (f + 1) * devices] for f in range(9)]
    put(0, part[0] + part[1])
    put(1, part[2] + part[3])
    put(2, part[4] + part[5])
    put(3, part[6] * 65536.0 + part[7] * 256.0 + part[8])


def pick(named, ranked, answers):
    devices = named.shape[0]
    high, low = split(answers)
    spread = dot(high, ranked) + dot(low, ranked)
    return jnp.concatenate(
        [
            jnp.sum(spread[c * devices : (c + 1) * devices] * named, axis=0, keepdims=True)
            for c in range(4)
        ],
        axis=0,
    )


def pair_forces(tiles, put, count, place):
    slots = tiles.shape[3]
    row = lax.broadcasted_iota(jnp.int32, (8, slots), 0)

    def one(index, carry):
        m, n = place(index)
        own = tiles[m + 1, n + 1]
        column = jnp.transpose(own)
        spread = [jnp.broadcast_to(column[:, d : d + 1], (slots, slots)) for d in range(3)]
        w_high, w_low, f_high, f_low = [], [], [], []
        for a in range(3):
            for b in range(3):
                shift = jnp.where(row == 0, a - 1.0, jnp.where(row == 1, b - 1.0, 0.0))
                other = tiles[m + a, n + b] + shift
                e = [spread[d] - other[d : d + 1] for d in range(3)]
                square = e[0] * e[0] + e[1] * e[1] + e[2] * e[2]
                s = square * lax.rsqrt(jnp.maximum(square, 1e-30))
                near = jnp.maximum(1.0 - s, 0.0)
                high, low = split(near * near * near)
                w_high.append(high)
                w_low.append(low)
                masked = other * other[7:8]
                high, low = split(jnp.concatenate([masked, masked * other[6:7]], axis=0))
                f_high.append(high)
                f_low.append(low)
        weights = jnp.concatenate(
            [jnp.concatenate(w_high, axis=1), jnp.concatenate(w_low, axis=1)], axis=0
        )
        factors = jnp.concatenate(
            [jnp.concatenate(f_high, axis=1), jnp.concatenate(f_low, axis=1)], axis=0
        )
        both = lax.dot_general(
            weights, factors, (((1,), (1,)), ((), ())), preferred_element_type=F32
        )
        both = jnp.transpose(both[:slots] + both[slots:])
        sums = both[:16] + both[16:]
        result = []
        for d in range(3):
            push = (
                own[6:7] * (own[d : d + 1] * sums[7:8] - sums[d : d + 1])
                + own[d : d + 1] * sums[6:7]
                - sums[8 + d : 9 + d]
            )
            drag = sums[3 + d : 4 + d] - own[3 + d : 4 + d] * sums[7:8]
            result.append((20.0 * FORCE_SCALE) * own[7:8] * (push + VISCOSITY * drag))
        put(m, n, result)
        return carry

    lax.fori_loop(0, count, one, 0)


def whole_kernel(
    grid,
    capacity,
    owner_ref,
    cell_ref,
    frac_ref,
    count_ref,
    fv,
    offset_ref,
    vel_ref,
    press_ref,
    tile_count_ref,
    fv_out,
    state_out,
    accel_out,
    slabs,
    fresh,
    stage,
    landed,
    corner_out,
    corner_in,
    y_low,
    y_up,
    y_up2,
    y_top,
    high,
    low,
    tiles,
    ask_out,
    ask_in,
    asked,
    reply_out,
    reply_in,
    near_send,
    near_recv,
    ask_send,
    ask_recv,
    reply_send,
    reply_recv,
    local_sem,
):
    grid_x, grid_y = grid
    devices = grid_x * grid_y
    gx, gy = lax.axis_index("gx"), lax.axis_index("gy")
    me = gx * grid_y + gy
    _, cells_x, cells_y, length = fresh.shape
    tiles_x, tiles_y, slots = press_ref.shape
    load = pltpu.make_async_copy(fv, slabs.at[:, 1 : 1 + cells_x], local_sem.at[0])
    load.start()

    for ref in (landed, corner_in, y_low, y_up, y_up2):
        ref[...] = jnp.zeros(ref.shape, ref.dtype)
    for x in (0, cells_x + 1, cells_x + 2):
        slabs[:, x] = jnp.zeros((4, cells_y, length), F32)
    for n in range(tiles_y + 2):
        tiles[0, n] = jnp.zeros(tiles.shape[2:], F32)
        tiles[tiles_x + 1, n] = jnp.zeros(tiles.shape[2:], F32)
    for m in range(tiles_x):
        tiles[m + 1, 0] = jnp.zeros(tiles.shape[2:], F32)
        tiles[m + 1, tiles_y + 1] = jnp.zeros(tiles.shape[2:], F32)
        for n in range(tiles_y):
            for d in range(3):
                tiles[m + 1, n + 1, d : d + 1] = offset_ref[d, m, n : n + 1]
                tiles[m + 1, n + 1, 3 + d : 4 + d] = vel_ref[d, m, n : n + 1]
            tiles[m + 1, n + 1, 6:7] = press_ref[m, n : n + 1]
            tiles[m + 1, n + 1, 7:8] = jnp.where(
                lax.broadcasted_iota(jnp.int32, (1, slots), 1) < tile_count_ref[m, n], 1.0, 0.0
            )

    def everyone(action):
        def step(p, carry):
            action(lax.rem(me + p, devices))
            return carry

        lax.fori_loop(1, devices, step, 0)

    def at(device):
        return {"gx": device // grid_y, "gy": lax.rem(device, grid_y)}

    barrier = pltpu.get_barrier_semaphore()
    everyone(
        lambda other: pl.semaphore_signal(
            barrier, inc=1, device_id=at(other), device_id_type=pl.DeviceIdType.MESH
        )
    )

    named, ranked = route(owner_ref[...], count_ref[0], devices)

    def put_ask(f, value):
        ask_out[:, f, :] = value

    pack(named, ranked, frac_ref[...], cell_ref[...], put_ask)
    load.wait()
    for x in range(cells_x):
        stage[0, :, x : x + 1, :] = slabs[:, x + 1, cells_y - 1 :, :]
        stage[1, :, x : x + 1, :] = slabs[:, x + 1, 0:1, :]
        stage[2, :, x : x + 1, :] = slabs[:, x + 1, 1:2, :]
    corner_out[...] = jnp.zeros(corner_out.shape, F32)
    corner_out[0, :, 0:1, :] = slabs[:, 1, 0:1, :]
    corner_out[0, :, 1:2, :] = slabs[:, 2, 0:1, :]
    corner_out[0, :, 2:3, :] = slabs[:, 1, 1:2, :]
    corner_out[1, :, 0:1, :] = slabs[:, cells_x, 0:1, :]
    corner_out[2, :, 0:1, :] = slabs[:, 1, cells_y - 1 :, :]
    ask_in[me] = ask_out[me]

    pl.semaphore_wait(barrier, devices - 1)

    def toward(order, source, target, dx, dy):
        copy = pltpu.make_async_remote_copy(
            src_ref=source,
            dst_ref=target,
            send_sem=near_send.at[order],
            recv_sem=near_recv.at[order],
            device_id={"gx": gx + dx, "gy": gy + dy},
            device_id_type=pl.DeviceIdType.MESH,
        )

        def inside(sign):
            ok = None
            for place, count, by in ((gx, grid_x, sign * dx), (gy, grid_y, sign * dy)):
                if by:
                    one = place + by < count if by > 0 else place + by >= 0
                    ok = one if ok is None else jnp.logical_and(ok, one)
            return ok

        return copy, inside(1), inside(-1)

    tx, ty = tiles_x, tiles_y
    field = [
        (fv.at[:, cells_x - 1 : cells_x], slabs.at[:, 0:1], 1, 0),
        (fv.at[:, 0:2], slabs.at[:, cells_x + 1 : cells_x + 3], -1, 0),
        (stage.at[0], landed.at[0], 0, 1),
        (stage.at[1:3], landed.at[1:3], 0, -1),
        (corner_out.at[0], corner_in.at[0], -1, -1),
        (corner_out.at[1], corner_in.at[1], 1, -1),
        (corner_out.at[2], corner_in.at[2], -1, 1),
    ]
    particles = [
        (tiles.at[tx, 1 : 1 + ty], tiles.at[0, 1 : 1 + ty], 1, 0),
        (tiles.at[1, 1 : 1 + ty], tiles.at[tx + 1, 1 : 1 + ty], -1, 0),
        (tiles.at[1 : 1 + tx, ty], tiles.at[1 : 1 + tx, 0], 0, 1),
        (tiles.at[1 : 1 + tx, 1], tiles.at[1 : 1 + tx, ty + 1], 0, -1),
        (tiles.at[tx, ty], tiles.at[0, 0], 1, 1),
        (tiles.at[tx, 1], tiles.at[0, ty + 1], 1, -1),
        (tiles.at[1, ty], tiles.at[tx + 1, 0], -1, 1),
        (tiles.at[1, 1], tiles.at[tx + 1, ty + 1], -1, -1),
    ]
    copies = [toward(i, *one) for i, one in enumerate(field + particles)]

    def exchange(out, into, send, recv, other, source):
        return pltpu.make_async_remote_copy(
            src_ref=out.at[other],
            dst_ref=into.at[source],
            send_sem=send.at[other],
            recv_sem=recv.at[source],
            device_id=at(other),
            device_id_type=pl.DeviceIdType.MESH,
        )

    for copy, to, _ in copies[: len(field)]:
        pl.when(to)(copy.start)
    everyone(lambda other: exchange(ask_out, ask_in, ask_send, ask_recv, other, me).start())
    for copy, to, _ in copies[len(field) :]:
        pl.when(to)(copy.start)

    def put_accel(m, n, result):
        for d in range(3):
            accel_out[d, m, pl.ds(n, 1), :] = result[d]

    inner = tiles_y - 2
    pair_forces(
        tiles, put_accel, (tiles_x - 2) * inner, lambda i: (1 + i // inner, 1 + lax.rem(i, inner))
    )

    for copy, _, source in copies[len(field) :]:
        pl.when(source)(copy.wait_recv)
    pair_forces(
        tiles,
        put_accel,
        2 * (tiles_x - 2),
        lambda i: (1 + i // 2, lax.rem(i, 2) * (tiles_y - 1)),
    )

    for copy, _, source in copies[: len(field)]:
        pl.when(source)(copy.wait_recv)
    y_low[:, 1 : 1 + cells_x] = landed[0]
    y_up[:, 1 : 1 + cells_x] = landed[1]
    y_up2[:, 1 : 1 + cells_x] = landed[2]
    y_up[:, cells_x + 1 : cells_x + 3] = corner_in[0, :, 0:2]
    y_up2[:, cells_x + 1 : cells_x + 2] = corner_in[0, :, 2:3]
    y_up[:, 0:1] = corner_in[1, :, 0:1]
    y_low[:, cells_x + 1 : cells_x + 2] = corner_in[2, :, 0:1]
    keep_x = jnp.where(gx < grid_x - 1, 1.0, 0.0)
    keep_y = jnp.where(gy < grid_y - 1, 1.0, 0.0)
    sweep_block(slabs, y_low, y_up, y_up2, y_top, fresh, high, low, keep_x, keep_y)
    store = pltpu.make_async_copy(fresh, fv_out, local_sem.at[1])
    store.start()

    everyone(lambda other: exchange(ask_out, ask_in, ask_send, ask_recv, me, other).wait_recv())
    share = LANES // capacity
    for q in range(devices // share):
        total = ask_in[q * share]
        for r in range(1, share):
            total = total + pltpu.roll(ask_in[q * share + r], r * capacity, 1)
        asked[:, q * LANES : (q + 1) * LANES] = total
    width = 512

    def put_reply(t, value):
        for q in range(width // LANES):
            part = value[:, q * LANES : (q + 1) * LANES]
            for r in range(share):
                turned = pltpu.roll(part, LANES - r * capacity, 1) if r else part
                reply_out[t * (width // capacity) + q * share + r] = turned

    interpolate(asked, high, low, fresh.shape, put_reply, width)
    everyone(
        lambda other: exchange(reply_out, reply_in, reply_send, reply_recv, other, me).start()
    )
    reply_in[me] = reply_out[me]

    pair_forces(
        tiles, put_accel, 2 * ty, lambda i: ((i // ty) * (tiles_x - 1), lax.rem(i, ty))
    )

    everyone(
        lambda other: exchange(
            reply_out, reply_in, reply_send, reply_recv, me, other
        ).wait_recv()
    )
    named, ranked = route(owner_ref[...], count_ref[0], devices)
    answers = jnp.concatenate([reply_in[:, c, :] for c in range(4)], axis=0)
    state_out[...] = pick(named, ranked, answers)

    for copy, to, _ in copies:
        pl.when(to)(copy.wait_send)
    everyone(lambda other: exchange(ask_out, ask_in, ask_send, ask_recv, other, me).wait_send())
    everyone(
        lambda other: exchange(reply_out, reply_in, reply_send, reply_recv, other, me).wait_send()
    )
    store.wait()


def per_device(
    fv_state,
    buffer_owner,
    buffer_cell,
    buffer_frac,
    buffer_count,
    sph_offset,
    sph_vel,
    sph_press,
    tile_count,
):
    grid = (lax.axis_size("gx"), lax.axis_size("gy"))
    devices = grid[0] * grid[1]
    _, cells_x, cells_y, length = fv_state.shape
    rows = buffer_cell.shape[0]
    capacity = 2 * rows // devices
    tiles_x, tiles_y, slots = sph_press.shape
    table = (cells_x + 1) * cells_y + 16
    mail = pltpu.VMEM((devices, 4, LANES), F32)
    dma = pltpu.SemaphoreType.DMA
    vmem = pl.BlockSpec(memory_space=pltpu.VMEM)
    scalars = pl.BlockSpec(memory_space=pltpu.SMEM)
    anywhere = pl.BlockSpec(memory_space=pl.ANY)
    return pl.pallas_call(
        functools.partial(whole_kernel, grid, capacity),
        out_shape=(
            jax.ShapeDtypeStruct(fv_state.shape, F32),
            jax.ShapeDtypeStruct((4, rows), F32),
            jax.ShapeDtypeStruct(sph_offset.shape, F32),
        ),
        in_specs=[vmem, vmem, vmem, scalars, anywhere, vmem, vmem, vmem, scalars],
        out_specs=(anywhere, vmem, vmem),
        scratch_shapes=[
            pltpu.VMEM((4, cells_x + 3, cells_y, length), F32),
            pltpu.VMEM((4, cells_x, cells_y, length), F32),
            pltpu.VMEM((3, 4, cells_x, length), F32),
            pltpu.VMEM((3, 4, cells_x, length), F32),
            pltpu.VMEM((3, 4, 8, length), F32),
            pltpu.VMEM((3, 4, 8, length), F32),
            pltpu.VMEM((4, 24, length), F32),
            pltpu.VMEM((4, 24, length), F32),
            pltpu.VMEM((4, 24, length), F32),
            pltpu.VMEM((4, 16, length), F32),
            pltpu.VMEM((4, table, length), BF16),
            pltpu.VMEM((4, table, length), BF16),
            pltpu.VMEM((tiles_x + 2, tiles_y + 2, 8, slots), F32),
            mail,
            mail,
            pltpu.VMEM((4, devices * capacity), F32),
            mail,
            mail,
            dma((15,)),
            dma((15,)),
            dma((devices,)),
            dma((devices,)),
            dma((devices,)),
            dma((devices,)),
            dma((2,)),
        ],
        compiler_params=pltpu.CompilerParams(
            collective_id=0, has_side_effects=True, vmem_limit_bytes=62 * 1024 * 1024
        ),
    )(
        buffer_owner.reshape(1, rows),
        buffer_cell.reshape(1, rows),
        buffer_frac,
        buffer_count,
        fv_state,
        sph_offset,
        sph_vel,
        sph_press,
        tile_count,
    )


def solution(mesh):
    return jax.shard_map(
        per_device,
        mesh=mesh,
        in_specs=(
            P(None, "gx", "gy", None),
            P(("gx", "gy"), None),
            P(("gx", "gy")),
            P(None, ("gx", "gy")),
            P(("gx", "gy")),
            P(None, "gx", "gy", None),
            P(None, "gx", "gy", None),
            P("gx", "gy", None),
            P("gx", "gy"),
        ),
        out_specs=(P(None, "gx", "gy", None), P(None, ("gx", "gy")), P(None, "gx", "gy", None)),
        check_vma=False,
    )
```

```python
import functools

import jax
import jax.numpy as jnp
from jax import lax
from jax.experimental import pallas as pl
from jax.experimental.pallas import tpu as pltpu
from jax.sharding import PartitionSpec as P

STEP_RATIO = 0.3
VISCOSITY = 0.02
FORCE_SCALE = 0.1
LANES = 128
F32 = jnp.float32
BF16 = jnp.bfloat16


def split(value):
    high = value.astype(BF16)
    return high, (value - high.astype(F32)).astype(BF16)


def dot(left, right):
    return jnp.dot(left, right, preferred_element_type=F32)


def sweep(centre, left, right, down, up):
    length = centre.shape[-1]
    lane = lax.broadcasted_iota(jnp.int32, centre.shape[1:], 1)
    below, above = [], []
    for c in range(4):
        below.append(jnp.where(lane == 0, 0.0, pltpu.roll(centre[c], 1, 1)))
        above.append(jnp.where(lane == length - 1, 0.0, pltpu.roll(centre[c], length - 1, 1)))
    lean = [
        (right[1] - left[1]) + (up[2] - down[2]) + (above[3] - below[3]),
        right[0] - left[0],
        up[0] - down[0],
        above[0] - below[0],
    ]
    result = []
    for c in range(4):
        around = (left[c] + right[c]) + (down[c] + up[c]) + (below[c] + above[c])
        result.append(
            (1.0 - 3.0 * STEP_RATIO) * centre[c] + (0.5 * STEP_RATIO) * (around - lean[c])
        )
    return result


def sweep_block(slabs, y_low, y_up, y_up2, y_top, fv_out, high, low, keep_x, keep_y):
    cells_x, cells_y = fv_out.shape[1], fv_out.shape[2]
    length = fv_out.shape[3]
    row = lax.broadcasted_iota(jnp.int32, (cells_y, length), 0)

    def slab(x, keep):
        centre = slabs[:, x + 1]
        first = y_low[:, pl.ds(x + 1, 1), :]
        last = y_up[:, pl.ds(x + 1, 1), :]
        down = [jnp.where(row == 0, first[c], pltpu.roll(centre[c], 1, 0)) for c in range(4)]
        up = [
            jnp.where(row == cells_y - 1, last[c], pltpu.roll(centre[c], cells_y - 1, 0))
            for c in range(4)
        ]
        new = sweep(centre, slabs[:, x], slabs[:, x + 2], down, up)
        y_top[:, pl.ds(x, 1), :] = centre[:, cells_y - 1 :, :]
        for c in range(4):
            value = new[c] if keep is None else new[c] * keep
            if keep is None:
                fv_out[c, x] = value
            high[c, pl.ds(x * cells_y, cells_y), :], low[c, pl.ds(x * cells_y, cells_y), :] = split(
                value
            )

    def step(x, carry):
        slab(x, None)
        return carry

    lax.fori_loop(0, cells_x, step, 0)
    slab(cells_x, keep_x)
    rows = 16
    y_top[:, cells_x + 1 :, :] = jnp.zeros((4, rows - cells_x - 1, length), F32)
    new = sweep(
        y_up[:, 1 : 1 + rows],
        y_up[:, 0:rows],
        y_up[:, 2 : 2 + rows],
        y_top[...],
        y_up2[:, 1 : 1 + rows],
    )
    edge = lax.broadcasted_iota(jnp.int32, (rows, length), 0)
    factor = jnp.where(edge < cells_x, keep_y, jnp.where(edge == cells_x, keep_x * keep_y, 0.0))
    start = (cells_x + 1) * cells_y
    for c in range(4):
        high[c, start : start + rows, :], low[c, start : start + rows, :] = split(new[c] * factor)


def blend(index, fraction, count, base=0):
    spot = lax.broadcasted_iota(jnp.int32, (count, index.shape[1]), 0) + base
    return jnp.where(spot == index, 1.0 - fraction, jnp.where(spot == index + 1, fraction, 0.0))


def interpolate(asked, high, low, shape, put, width):
    _, cells_x, cells_y, length = shape
    rows = high.shape[1]

    def tile(t, carry):
        lanes = pl.ds(pl.multiple_of(t * width, width), width)
        cell = asked[3:4, lanes].astype(jnp.int32)
        k = cell % length
        plane = cell // length
        spot = lax.broadcasted_iota(jnp.int32, (length, width), 0)
        c = asked[2:3, lanes]
        w_high, w_low = split(blend(k, c, length))
        t_high = high[...].reshape(4 * rows, length)
        t_low = low[...].reshape(4 * rows, length)
        mixed = dot(t_high, w_high) + dot(t_low, w_high) + dot(t_high, w_low)
        weight_y = blend(plane % cells_y, asked[1:2, lanes], cells_y)
        last_y = jnp.where(plane % cells_y == cells_y - 1, asked[1:2, lanes], 0.0)
        weight_x = blend(plane // cells_y, asked[0:1, lanes], 16)
        out = []
        for channel in range(4):
            first = channel * rows
            total = jnp.zeros((cells_y, width), F32)
            for x in range(cells_x + 1):
                part = mixed[first + x * cells_y : first + (x + 1) * cells_y]
                total = total + weight_x[x : x + 1] * part
            edge = mixed[first + rows - 16 : first + rows] * weight_x
            out.append(
                jnp.sum(total * weight_y, axis=0, keepdims=True)
                + last_y * jnp.sum(edge, axis=0, keepdims=True)
            )
        put(t, jnp.concatenate(out, axis=0))
        return carry

    lax.fori_loop(0, asked.shape[1] // width, tile, 0)


def route(owner, count, devices):
    rows = owner.shape[1]
    live = lax.broadcasted_iota(jnp.int32, (1, rows), 1) < count
    place = lax.broadcasted_iota(jnp.int32, (devices, rows), 0)
    named = jnp.where((place == owner) & live, 1.0, 0.0)
    blocks = rows // LANES
    stacked = jnp.concatenate(
        [named[:, b * LANES : (b + 1) * LANES] for b in range(blocks)], axis=0
    ).astype(BF16)
    source = lax.broadcasted_iota(jnp.int32, (LANES, 2 * LANES), 0)
    target = lax.broadcasted_iota(jnp.int32, (LANES, 2 * LANES), 1)
    ladder = jnp.where((source < target) | (target >= LANES), 1.0, 0.0).astype(BF16)
    tallies = dot(stacked, ladder)
    running = jnp.zeros((devices, LANES), F32)
    ranks = []
    for b in range(blocks):
        part = tallies[b * devices : (b + 1) * devices]
        earlier = part[:, :LANES] + running
        running = running + part[:, LANES:]
        ranks.append(
            jnp.sum(earlier * named[:, b * LANES : (b + 1) * LANES], axis=0, keepdims=True)
        )
    rank = jnp.concatenate(ranks, axis=1).astype(jnp.int32)
    slot = lax.broadcasted_iota(jnp.int32, (LANES, rows), 0)
    ranked = jnp.where((slot == rank) & live, 1.0, 0.0).astype(BF16)
    return named, ranked


def pack(named, ranked, frac, cell, put):
    devices = named.shape[0]
    fields = []
    for d in range(3):
        high = frac[d : d + 1].astype(BF16).astype(F32)
        fields += [high, frac[d : d + 1] - high]
    fields += [
        (cell // 65536).astype(F32),
        (cell // 256 % 256).astype(F32),
        (cell % 256).astype(F32),
    ]
    stacked = jnp.concatenate([(named * field).astype(BF16) for field in fields], axis=0)
    sent = lax.dot_general(
        stacked, ranked, (((1,), (1,)), ((), ())), preferred_element_type=F32
    )
    part = [sent[f * devices : (f + 1) * devices] for f in range(9)]
    put(0, part[0] + part[1])
    put(1, part[2] + part[3])
    put(2, part[4] + part[5])
    put(3, part[6] * 65536.0 + part[7] * 256.0 + part[8])


def pick(named, ranked, answers):
    devices = named.shape[0]
    high, low = split(answers)
    spread = dot(high, ranked) + dot(low, ranked)
    return jnp.concatenate(
        [
            jnp.sum(spread[c * devices : (c + 1) * devices] * named, axis=0, keepdims=True)
            for c in range(4)
        ],
        axis=0,
    )


def pair_forces(tiles, put, count, place):
    slots = tiles.shape[3]
    row = lax.broadcasted_iota(jnp.int32, (8, slots), 0)

    def one(index, carry):
        m, n = place(index)
        own = tiles[m + 1, n + 1]
        column = jnp.transpose(own)
        spread = [jnp.broadcast_to(column[:, d : d + 1], (slots, slots)) for d in range(3)]
        w_high, w_low, f_high, f_low = [], [], [], []
        for a in range(3):
            for b in range(3):
                shift = jnp.where(row == 0, a - 1.0, jnp.where(row == 1, b - 1.0, 0.0))
                other = tiles[m + a, n + b] + shift
                e = [spread[d] - other[d : d + 1] for d in range(3)]
                square = e[0] * e[0] + e[1] * e[1] + e[2] * e[2]
                s = square * lax.rsqrt(jnp.maximum(square, 1e-30))
                near = jnp.maximum(1.0 - s, 0.0)
                high, low = split(near * near * near)
                w_high.append(high)
                w_low.append(low)
                masked = other * other[7:8]
                high, low = split(jnp.concatenate([masked, masked * other[6:7]], axis=0))
                f_high.append(high)
                f_low.append(low)
        weights = jnp.concatenate(
            [jnp.concatenate(w_high, axis=1), jnp.concatenate(w_low, axis=1)], axis=0
        )
        factors = jnp.concatenate(
            [jnp.concatenate(f_high, axis=1), jnp.concatenate(f_low, axis=1)], axis=0
        )
        both = lax.dot_general(
            weights, factors, (((1,), (1,)), ((), ())), preferred_element_type=F32
        )
        both = jnp.transpose(both[:slots] + both[slots:])
        sums = both[:16] + both[16:]
        result = []
        for d in range(3):
            push = (
                own[6:7] * (own[d : d + 1] * sums[7:8] - sums[d : d + 1])
                + own[d : d + 1] * sums[6:7]
                - sums[8 + d : 9 + d]
            )
            drag = sums[3 + d : 4 + d] - own[3 + d : 4 + d] * sums[7:8]
            result.append((20.0 * FORCE_SCALE) * own[7:8] * (push + VISCOSITY * drag))
        put(m, n, result)
        return carry

    lax.fori_loop(0, count, one, 0)


def whole_kernel(
    grid,
    capacity,
    owner_ref,
    cell_ref,
    frac_ref,
    count_ref,
    fv,
    offset_ref,
    vel_ref,
    press_ref,
    tile_count_ref,
    fv_out,
    state_out,
    accel_out,
    slabs,
    fresh,
    stage,
    landed,
    corner_out,
    corner_in,
    y_low,
    y_up,
    y_up2,
    y_top,
    high,
    low,
    tiles,
    ask_out,
    ask_in,
    asked,
    reply_out,
    reply_in,
    near_send,
    near_recv,
    ask_send,
    ask_recv,
    reply_send,
    reply_recv,
    local_sem,
):
    grid_x, grid_y = grid
    devices = grid_x * grid_y
    gx, gy = lax.axis_index("gx"), lax.axis_index("gy")
    me = gx * grid_y + gy
    _, cells_x, cells_y, length = fresh.shape
    tiles_x, tiles_y, slots = press_ref.shape
    load = pltpu.make_async_copy(fv, slabs.at[:, 1 : 1 + cells_x], local_sem.at[0])
    load.start()

    for ref in (landed, corner_in, y_low, y_up, y_up2):
        ref[...] = jnp.zeros(ref.shape, ref.dtype)
    for x in (0, cells_x + 1, cells_x + 2):
        slabs[:, x] = jnp.zeros((4, cells_y, length), F32)
    for n in range(tiles_y + 2):
        tiles[0, n] = jnp.zeros(tiles.shape[2:], F32)
        tiles[tiles_x + 1, n] = jnp.zeros(tiles.shape[2:], F32)
    for m in range(tiles_x):
        tiles[m + 1, 0] = jnp.zeros(tiles.shape[2:], F32)
        tiles[m + 1, tiles_y + 1] = jnp.zeros(tiles.shape[2:], F32)
        for n in range(tiles_y):
            for d in range(3):
                tiles[m + 1, n + 1, d : d + 1] = offset_ref[d, m, n : n + 1]
                tiles[m + 1, n + 1, 3 + d : 4 + d] = vel_ref[d, m, n : n + 1]
            tiles[m + 1, n + 1, 6:7] = press_ref[m, n : n + 1]
            tiles[m + 1, n + 1, 7:8] = jnp.where(
                lax.broadcasted_iota(jnp.int32, (1, slots), 1) < tile_count_ref[m, n], 1.0, 0.0
            )

    def everyone(action):
        def step(p, carry):
            action(lax.rem(me + p, devices))
            return carry

        lax.fori_loop(1, devices, step, 0)

    def at(device):
        return {"gx": device // grid_y, "gy": lax.rem(device, grid_y)}

    barrier = pltpu.get_barrier_semaphore()
    everyone(
        lambda other: pl.semaphore_signal(
            barrier, inc=1, device_id=at(other), device_id_type=pl.DeviceIdType.MESH
        )
    )

    named, ranked = route(owner_ref[...], count_ref[0], devices)

    def put_ask(f, value):
        ask_out[:, f, :] = value

    pack(named, ranked, frac_ref[...], cell_ref[...], put_ask)
    ask_in[me] = ask_out[me]

    pl.semaphore_wait(barrier, devices - 1)

    def toward(order, source, target, dx, dy):
        copy = pltpu.make_async_remote_copy(
            src_ref=source,
            dst_ref=target,
            send_sem=near_send.at[order],
            recv_sem=near_recv.at[order],
            device_id={"gx": gx + dx, "gy": gy + dy},
            device_id_type=pl.DeviceIdType.MESH,
        )

        def inside(sign):
            ok = None
            for place, count, by in ((gx, grid_x, sign * dx), (gy, grid_y, sign * dy)):
                if by:
                    one = place + by < count if by > 0 else place + by >= 0
                    ok = one if ok is None else jnp.logical_and(ok, one)
            return ok

        return copy, inside(1), inside(-1)

    tx, ty = tiles_x, tiles_y
    field = [
        (fv.at[:, cells_x - 1 : cells_x], slabs.at[:, 0:1], 1, 0),
        (fv.at[:, 0:2], slabs.at[:, cells_x + 1 : cells_x + 3], -1, 0),
        (stage.at[0], landed.at[0], 0, 1),
        (stage.at[1:3], landed.at[1:3], 0, -1),
        (corner_out.at[0], corner_in.at[0], -1, -1),
        (corner_out.at[1], corner_in.at[1], 1, -1),
        (corner_out.at[2], corner_in.at[2], -1, 1),
    ]
    particles = [
        (tiles.at[tx, 1 : 1 + ty], tiles.at[0, 1 : 1 + ty], 1, 0),
        (tiles.at[1, 1 : 1 + ty], tiles.at[tx + 1, 1 : 1 + ty], -1, 0),
        (tiles.at[1 : 1 + tx, ty], tiles.at[1 : 1 + tx, 0], 0, 1),
        (tiles.at[1 : 1 + tx, 1], tiles.at[1 : 1 + tx, ty + 1], 0, -1),
        (tiles.at[tx, ty], tiles.at[0, 0], 1, 1),
        (tiles.at[tx, 1], tiles.at[0, ty + 1], 1, -1),
        (tiles.at[1, ty], tiles.at[tx + 1, 0], -1, 1),
        (tiles.at[1, 1], tiles.at[tx + 1, ty + 1], -1, -1),
    ]
    copies = [toward(i, *one) for i, one in enumerate(field + particles)]

    def exchange(out, into, send, recv, other, source):
        return pltpu.make_async_remote_copy(
            src_ref=out.at[other],
            dst_ref=into.at[source],
            send_sem=send.at[other],
            recv_sem=recv.at[source],
            device_id=at(other),
            device_id_type=pl.DeviceIdType.MESH,
        )

    for copy, to, _ in copies[len(field) :]:
        pl.when(to)(copy.start)
    for copy, to, _ in copies[:2]:
        pl.when(to)(copy.start)
    load.wait()
    for x in range(cells_x):
        stage[0, :, x : x + 1, :] = slabs[:, x + 1, cells_y - 1 :, :]
        stage[1, :, x : x + 1, :] = slabs[:, x + 1, 0:1, :]
        stage[2, :, x : x + 1, :] = slabs[:, x + 1, 1:2, :]
    corner_out[...] = jnp.zeros(corner_out.shape, F32)
    corner_out[0, :, 0:1, :] = slabs[:, 1, 0:1, :]
    corner_out[0, :, 1:2, :] = slabs[:, 2, 0:1, :]
    corner_out[0, :, 2:3, :] = slabs[:, 1, 1:2, :]
    corner_out[1, :, 0:1, :] = slabs[:, cells_x, 0:1, :]
    corner_out[2, :, 0:1, :] = slabs[:, 1, cells_y - 1 :, :]
    for copy, to, _ in copies[2 : len(field)]:
        pl.when(to)(copy.start)
    everyone(lambda other: exchange(ask_out, ask_in, ask_send, ask_recv, other, me).start())

    def put_accel(m, n, result):
        for d in range(3):
            accel_out[d, m, pl.ds(n, 1), :] = result[d]

    inner = tiles_y - 2
    pair_forces(
        tiles, put_accel, (tiles_x - 2) * inner, lambda i: (1 + i // inner, 1 + lax.rem(i, inner))
    )

    for copy, _, source in copies[len(field) :]:
        pl.when(source)(copy.wait_recv)
    pair_forces(
        tiles,
        put_accel,
        2 * (tiles_x - 2),
        lambda i: (1 + i // 2, lax.rem(i, 2) * (tiles_y - 1)),
    )

    for copy, _, source in copies[: len(field)]:
        pl.when(source)(copy.wait_recv)
    y_low[:, 1 : 1 + cells_x] = landed[0]
    y_up[:, 1 : 1 + cells_x] = landed[1]
    y_up2[:, 1 : 1 + cells_x] = landed[2]
    y_up[:, cells_x + 1 : cells_x + 3] = corner_in[0, :, 0:2]
    y_up2[:, cells_x + 1 : cells_x + 2] = corner_in[0, :, 2:3]
    y_up[:, 0:1] = corner_in[1, :, 0:1]
    y_low[:, cells_x + 1 : cells_x + 2] = corner_in[2, :, 0:1]
    keep_x = jnp.where(gx < grid_x - 1, 1.0, 0.0)
    keep_y = jnp.where(gy < grid_y - 1, 1.0, 0.0)
    sweep_block(slabs, y_low, y_up, y_up2, y_top, fresh, high, low, keep_x, keep_y)
    store = pltpu.make_async_copy(fresh, fv_out, local_sem.at[1])
    store.start()

    everyone(lambda other: exchange(ask_out, ask_in, ask_send, ask_recv, me, other).wait_recv())
    share = LANES // capacity
    for q in range(devices // share):
        total = ask_in[q * share]
        for r in range(1, share):
            total = total + pltpu.roll(ask_in[q * share + r], r * capacity, 1)
        asked[:, q * LANES : (q + 1) * LANES] = total
    width = 512

    def put_reply(t, value):
        for q in range(width // LANES):
            part = value[:, q * LANES : (q + 1) * LANES]
            for r in range(share):
                turned = pltpu.roll(part, LANES - r * capacity, 1) if r else part
                reply_out[t * (width // capacity) + q * share + r] = turned

    interpolate(asked, high, low, fresh.shape, put_reply, width)
    everyone(
        lambda other: exchange(reply_out, reply_in, reply_send, reply_recv, other, me).start()
    )
    reply_in[me] = reply_out[me]

    pair_forces(
        tiles, put_accel, 2 * ty, lambda i: ((i // ty) * (tiles_x - 1), lax.rem(i, ty))
    )

    everyone(
        lambda other: exchange(
            reply_out, reply_in, reply_send, reply_recv, me, other
        ).wait_recv()
    )
    answers = jnp.concatenate([reply_in[:, c, :] for c in range(4)], axis=0)
    state_out[...] = pick(named, ranked, answers)

    for copy, to, _ in copies:
        pl.when(to)(copy.wait_send)
    everyone(lambda other: exchange(ask_out, ask_in, ask_send, ask_recv, other, me).wait_send())
    everyone(
        lambda other: exchange(reply_out, reply_in, reply_send, reply_recv, other, me).wait_send()
    )
    store.wait()


def per_device(
    fv_state,
    buffer_owner,
    buffer_cell,
    buffer_frac,
    buffer_count,
    sph_offset,
    sph_vel,
    sph_press,
    tile_count,
):
    grid = (lax.axis_size("gx"), lax.axis_size("gy"))
    devices = grid[0] * grid[1]
    _, cells_x, cells_y, length = fv_state.shape
    rows = buffer_cell.shape[0]
    capacity = 2 * rows // devices
    tiles_x, tiles_y, slots = sph_press.shape
    table = (cells_x + 1) * cells_y + 16
    mail = pltpu.VMEM((devices, 4, LANES), F32)
    dma = pltpu.SemaphoreType.DMA
    vmem = pl.BlockSpec(memory_space=pltpu.VMEM)
    scalars = pl.BlockSpec(memory_space=pltpu.SMEM)
    anywhere = pl.BlockSpec(memory_space=pl.ANY)
    return pl.pallas_call(
        functools.partial(whole_kernel, grid, capacity),
        out_shape=(
            jax.ShapeDtypeStruct(fv_state.shape, F32),
            jax.ShapeDtypeStruct((4, rows), F32),
            jax.ShapeDtypeStruct(sph_offset.shape, F32),
        ),
        in_specs=[vmem, vmem, vmem, scalars, pl.BlockSpec(memory_space=pltpu.HBM), vmem, vmem, vmem, scalars],
        out_specs=(anywhere, vmem, vmem),
        scratch_shapes=[
            pltpu.VMEM((4, cells_x + 3, cells_y, length), F32),
            pltpu.VMEM((4, cells_x, cells_y, length), F32),
            pltpu.VMEM((3, 4, cells_x, length), F32),
            pltpu.VMEM((3, 4, cells_x, length), F32),
            pltpu.VMEM((3, 4, 4, length), F32),
            pltpu.VMEM((3, 4, 4, length), F32),
            pltpu.VMEM((4, 24, length), F32),
            pltpu.VMEM((4, 24, length), F32),
            pltpu.VMEM((4, 24, length), F32),
            pltpu.VMEM((4, 16, length), F32),
            pltpu.VMEM((4, table, length), BF16),
            pltpu.VMEM((4, table, length), BF16),
            pltpu.VMEM((tiles_x + 2, tiles_y + 2, 8, slots), F32),
            mail,
            mail,
            pltpu.VMEM((4, devices * capacity), F32),
            mail,
            mail,
            dma((15,)),
            dma((15,)),
            dma((devices,)),
            dma((devices,)),
            dma((devices,)),
            dma((devices,)),
            dma((2,)),
        ],
        compiler_params=pltpu.CompilerParams(
            collective_id=0, has_side_effects=True, vmem_limit_bytes=62 * 1024 * 1024
        ),
    )(
        buffer_owner.reshape(1, rows),
        buffer_cell.reshape(1, rows),
        buffer_frac,
        buffer_count,
        fv_state,
        sph_offset,
        sph_vel,
        sph_press,
        tile_count,
    )


def solution(mesh):
    return jax.shard_map(
        per_device,
        mesh=mesh,
        in_specs=(
            P(None, "gx", "gy", None),
            P(("gx", "gy"), None),
            P(("gx", "gy")),
            P(None, ("gx", "gy")),
            P(("gx", "gy")),
            P(None, "gx", "gy", None),
            P(None, "gx", "gy", None),
            P("gx", "gy", None),
            P("gx", "gy"),
        ),
        out_specs=(P(None, "gx", "gy", None), P(None, ("gx", "gy")), P(None, "gx", "gy", None)),
        check_vma=False,
    )
```
